32 devices in a mesh: ab: 4 (over y, core), cd: 8 (over z, x).
Axes of the slice: x: 2, y: 2, z: 4, core: 2. Of those that a mesh axis runs over, the one named last changes fastest.
Arguments:
- pair_values: bfloat16 [8192, 16384], P('ab', 'cd'), may hold values from -0.0625 to 0.0625
- amplitudes: bfloat16 [64, 800, 800], P('ab', 'cd'), may hold values from -6 to 6
- cd_first: int32 [16384], P('cd'), may hold values from 0 to 799, as said below
- cd_second: int32 [16384], P('cd'), may hold values from 0 to 799, as said below
- live_cols: int32 [8], P('cd'), may hold values from 512 to 2048, as said below
Outputs:
- ladder: bfloat16 [64, 8192], P(None, ('ab', 'cd'))
The draws below stay inside these ranges and needn't reach their ends.
Inputs may be any that keep to these rules, and one draw needn't show every extreme that they name: `cd_first`: slot n lies in slab s = n // 2048 and its c lies in orbitals s * 100 to (s + 1) * 100 - 1. cd_second[n] >= cd_first[n] for every slot. `live_cols`: slots 0 and 1 of every slab are live.
All inputs are finite; a program needn't handle non-finite values.
Results may differ from the reference program's by a relative error of at most 0.0051.
Values may be sent and summed in bfloat16 or wider, within the bound.
No kernel may reach another device: no remote copies, remote signals or barrier semaphores. Data moves between devices by JAX's collectives and lax.ppermute only.
A program may use at most 64 MiB of HBM per device.

```python
import jax
import jax.numpy as jnp
from jax import lax

NV = 800
PAIRS = 64
AB_DEV = 2048
COLS = 2048
CB = 100
NAB = 8192
NCOL = 16384
SLABS = 8


def pair_lists(key):
    base = jax.random.fold_in(key, 11)
    key_one, key_two, key_three = jax.random.split(base, 3)
    index = jnp.arange(NCOL, dtype=jnp.int32)
    slot = index % COLS
    owner = index // COLS
    local = jax.random.randint(key_one, (NCOL,), 0, CB, dtype=jnp.int32)
    local = jnp.where(slot == 0, 0, jnp.where(slot == 1, CB - 1, local))
    first = owner * CB + local
    offset = jax.random.randint(key_two, (NCOL,), 0, NV - first, dtype=jnp.int32)
    diagonal = jax.random.randint(key_three, (NCOL,), 0, 8, dtype=jnp.int32) == 0
    second = jnp.where(diagonal, first, first + offset)
    second = jnp.where(slot == 0, first, jnp.where(slot == 1, NV - 1, second))
    return (first.astype(jnp.int32), second.astype(jnp.int32))


def draw_cd_first(key, part):
    return pair_lists(key)[0]


def draw_cd_second(key, part):
    return pair_lists(key)[1]


def draw_live_cols(key, part):
    base = jax.random.fold_in(key, 23)
    key_one, key_two, key_three = jax.random.split(base, 3)
    counts = jax.random.randint(key_one, (SLABS,), COLS // 4, COLS + 1, dtype=jnp.int32)
    fullest = jax.random.randint(key_two, (), 0, SLABS, dtype=jnp.int32)
    lightest = (fullest + 1 + jax.random.randint(key_three, (), 0, SLABS - 1, dtype=jnp.int32)) % SLABS
    index = jnp.arange(SLABS, dtype=jnp.int32)
    counts = jnp.where(index == fullest, COLS, counts)
    counts = jnp.where(index == lightest, COLS // 4, counts)
    return counts.astype(jnp.int32)


def raised(values, rng, source, target, blocks, factor):
    def block_of(axis_at):
        return (jnp.arange(values.shape[axis_at]) // (values.shape[axis_at] // blocks)).reshape((-1,) + (1,) * (values.ndim - 1 - axis_at))

    near = jax.random.permutation(rng, blocks)[block_of(target)]
    second = (block_of(target) + blocks // 2) % blocks
    return jnp.where((block_of(source) == near) | (block_of(source) == second), factor * values, values)


def block_scale(stream_key, shape, pieces, low, top_value):
    def one(axis_at, parts):
        heights = jax.random.uniform(jax.random.fold_in(jax.random.fold_in(stream_key, 6), axis_at), (parts,), jnp.float32, low / len(pieces), top_value / len(pieces))
        return jnp.repeat(jnp.exp(heights), shape[axis_at] // parts).reshape((-1,) + (1,) * (len(shape) - axis_at - 1))

    level = one(*pieces[0])
    for cut in pieces[1:]:
        level = level * one(*cut)
    return level


def normal_values(rng, extent, deviation, bound, pieces=(), held_as=jnp.bfloat16):
    values = jax.random.normal(rng, extent, jnp.float32) * deviation
    if len(pieces) > 0:
        values = block_scale(rng, extent, pieces, -0.22, 0.18) * values
    return jnp.clip(values, min=-bound, max=bound).astype(held_as)


def noise_with(stream_key, shape, scale, bound, shards, heavy, kind=jnp.bfloat16):
    drawn = scale * jax.random.normal(stream_key, shape, jnp.float32)
    if shards:
        drawn = drawn * block_scale(stream_key, shape, shards, -0.22, 0.18)
    return jnp.clip(raised(drawn, jax.random.fold_in(stream_key, 3), *heavy), -bound, bound).astype(kind)


def setup_inputs(seed: int = 0) -> dict:
    key_of = jax.random.split(jax.random.key(seed), 6)
    return {
        "pair_values": noise_with(key_of[0], (NAB, NCOL), NCOL ** -0.5, 0.0625, ((0, 4), (1, 8)), (1, 0, 8, 2.0)),
        "amplitudes": normal_values(key_of[1], (PAIRS, NV, NV), 1.0, 6.0, ((0, 4), (1, 8))),
        "cd_first": draw_cd_first(jax.random.fold_in(key_of[5], 71), 0),
        "cd_second": draw_cd_second(jax.random.fold_in(key_of[5], 71), 0),
        "live_cols": draw_live_cols(jax.random.fold_in(key_of[5], 71), 0),
    }


def reference(pair_values, amplitudes, cd_first, cd_second, live_cols):
    ncol = cd_first.shape[0]
    direct = amplitudes[:, cd_first, cd_second].astype(jnp.float32)
    crossed = amplitudes[:, cd_second, cd_first].astype(jnp.float32)
    slot = jnp.arange(ncol, dtype=jnp.int32) % COLS
    owner = jnp.arange(ncol, dtype=jnp.int32) // COLS
    live = (slot < live_cols[owner]).astype(jnp.float32)
    half = jnp.where(cd_first == cd_second, jnp.float32(0.5), jnp.float32(1.0)).astype(jnp.float32)
    weight = half * live
    packed = ((direct + crossed) * weight[None, :]).astype(jnp.bfloat16)
    blocks = pair_values.reshape(NAB // AB_DEV, AB_DEV, ncol)

    def one_block(values_block):
        return lax.dot_general(packed, values_block, (((1,), (1,)), ((), ())), preferred_element_type=jnp.float32)

    result = lax.map(one_block, blocks)
    return jnp.transpose(result, (1, 0, 2)).reshape(PAIRS, NAB).astype(jnp.bfloat16)
```

```python
import functools

import jax
import jax.numpy as jnp
from jax import lax
from jax.experimental import pallas as pl
from jax.experimental.pallas import tpu as pltpu
from jax.sharding import PartitionSpec as P

LANES = 128
VMEM_LIMIT = 48 * 1024 * 1024


def chunk_of(columns):
    return min(columns, 512)


def one_hot(keys, depth):
    rows = lax.broadcasted_iota(jnp.int32, (depth, keys.shape[1]), 0)
    return jnp.where(rows == keys, 1.0, 0.0).astype(jnp.bfloat16)


def picked(groups, sums, pairs, total):
    for g in range(sums.shape[0] // pairs):
        total = jnp.where(groups == g, sums[g * pairs : (g + 1) * pairs], total)
    return total


def direct_kernel(slabs, orbits, pairs, table_ref, first_ref, second_ref, aligned_ref, direct_ref):
    rows = orbits * pairs
    for s in range(slabs):
        aligned_ref[s, :, :] = jnp.concatenate(
            [
                table_ref[:, s * orbits : (s + 1) * orbits],
                jnp.zeros((rows, LANES - orbits), jnp.bfloat16),
            ],
            axis=1,
        )
    columns = first_ref.shape[1]
    width = chunk_of(columns)

    def step(i, carry):
        at = pl.ds(pl.multiple_of(i * width, width), width)
        second = second_ref[:, at]
        owner = second // orbits
        keys = owner * LANES + (second - owner * orbits)
        hot = one_hot(keys, slabs * LANES)
        sums = jnp.dot(
            jnp.concatenate([aligned_ref[s] for s in range(slabs)], axis=1),
            hot,
            preferred_element_type=jnp.float32,
        )
        zero = jnp.zeros((pairs, width), jnp.float32)
        direct_ref[:, at] = picked(first_ref[:, at], sums, pairs, zero).astype(jnp.bfloat16)
        return carry

    lax.fori_loop(0, columns // width, step, 0)


def crossed_kernel(slabs, orbits, pairs, me_ref, aligned_ref, key_ref, group_ref, crossed_ref):
    columns = key_ref.shape[2]
    width = chunk_of(columns)
    me = me_ref[0]
    halves = orbits // 2

    def slab_step(s, carry):
        def step(i, inner):
            at = pl.ds(pl.multiple_of(i * width, width), width)
            hot = one_hot(key_ref[s, :, at], 2 * LANES)
            even = aligned_ref[s, :, 0].reshape(halves * pairs, LANES)
            odd = aligned_ref[s, :, 1].reshape(halves * pairs, LANES)
            sums = jnp.dot(
                jnp.concatenate([even, odd], axis=1), hot, preferred_element_type=jnp.float32
            )
            zero = jnp.zeros((pairs, width), jnp.float32)
            crossed_ref[s, :, at] = picked(group_ref[s, :, at], sums, pairs, zero).astype(
                jnp.bfloat16
            )
            return inner

        return lax.fori_loop(0, columns // width, step, carry)

    def blank(s, carry):
        crossed_ref[s] = jnp.zeros(crossed_ref.shape[1:], jnp.bfloat16)
        return carry

    lax.fori_loop(0, me + 1, slab_step, 0)
    lax.fori_loop(me + 1, slabs, blank, 0)


def ladder_kernel(slabs, packed_ref, values_ref, out_ref):
    width = out_ref.shape[2]
    out_ref[0] = lax.dot_general(
        packed_ref[...],
        values_ref[...],
        (((1,), (1,)), ((), ())),
        preferred_element_type=jnp.float32,
    ).astype(jnp.bfloat16)


def on_device(pair_values, amplitudes, cd_first, cd_second, live_cols):
    slab = lax.axis_index("cd")
    slabs = lax.axis_size("cd")
    blocks = lax.axis_size("ab")
    pair_block, orbits, orbitals = amplitudes.shape
    columns = cd_first.shape[0]
    rows = pair_values.shape[0]
    pairs = -(-pair_block // 16) * 16
    table = jnp.transpose(amplitudes, (1, 0, 2))
    if pairs != pair_block:
        table = jnp.pad(table, ((0, 0), (0, pairs - pair_block), (0, 0)))
    table = table.reshape(orbits * pairs, orbitals)
    vmem = pl.BlockSpec(memory_space=pltpu.VMEM)
    params = pltpu.CompilerParams(vmem_limit_bytes=VMEM_LIMIT)

    local_first = cd_first - slab * orbits
    coded = (local_first * orbitals + cd_second).reshape(1, columns // LANES, LANES)
    coded = lax.all_to_all(
        jnp.broadcast_to(coded, (slabs,) + coded.shape[1:]), "cd", split_axis=0, concat_axis=0, tiled=True
    )
    aligned, direct = pl.pallas_call(
        functools.partial(direct_kernel, slabs, orbits, pairs),
        out_shape=(
            jax.ShapeDtypeStruct((slabs, orbits * pairs, LANES), jnp.bfloat16),
            jax.ShapeDtypeStruct((pairs, columns), jnp.bfloat16),
        ),
        in_specs=[vmem] * 3,
        out_specs=(vmem, vmem),
        compiler_params=params,
        cost_estimate=pl.CostEstimate(
            flops=2 * orbits * pairs * slabs * LANES * columns, bytes_accessed=6_000_000, transcendentals=0
        ),
        name="direct",
    )(table, local_first.reshape(1, columns), cd_second.reshape(1, columns))

    coded = coded.reshape(slabs, 1, columns)
    first = coded // orbitals
    second = coded - first * orbitals - slab * orbits
    keys = jnp.where(second % 2 == 0, first, first + LANES)
    groups = second >> 1
    crossed = pl.pallas_call(
        functools.partial(crossed_kernel, slabs, orbits, pairs),
        out_shape=jax.ShapeDtypeStruct((slabs, pairs, columns), jnp.bfloat16),
        in_specs=[pl.BlockSpec(memory_space=pltpu.SMEM)] + [vmem] * 3,
        out_specs=vmem,
        compiler_params=params,
        cost_estimate=pl.CostEstimate(
            flops=slabs * orbits * pairs * 2 * LANES * columns, bytes_accessed=6_000_000, transcendentals=0
        ),
        name="crossed",
    )(
        slab.astype(jnp.int32).reshape(1),
        aligned.reshape(slabs, orbits // 2, 2, pairs, LANES),
        keys,
        groups,
    )
    crossed = lax.all_to_all(crossed, "cd", split_axis=0, concat_axis=0, tiled=True)
    crossed = jnp.sum(crossed.astype(jnp.float32), axis=0)

    slots = jnp.arange(columns, dtype=jnp.int32)
    live = (slots < live_cols[0]).astype(jnp.float32)
    half = jnp.where(cd_first == cd_second, jnp.float32(0.5), jnp.float32(1.0))
    packed = ((direct.astype(jnp.float32) + crossed) * (half * live)[None, :]).astype(jnp.bfloat16)
    packed = lax.all_gather(packed[:pair_block], "ab", axis=0, tiled=True)

    width = rows // slabs
    partial_sums = pl.pallas_call(
        functools.partial(ladder_kernel, slabs),
        out_shape=jax.ShapeDtypeStruct((slabs, blocks * pair_block, width), jnp.bfloat16),
        grid=(slabs,),
        in_specs=[
            pl.BlockSpec((blocks * pair_block, columns), lambda i: (0, 0)),
            pl.BlockSpec((width, columns), lambda i: (i, 0)),
        ],
        out_specs=pl.BlockSpec((1, blocks * pair_block, width), lambda i: (i, 0, 0)),
        compiler_params=params,
        cost_estimate=pl.CostEstimate(
            flops=2 * blocks * pair_block * columns * rows, bytes_accessed=rows * columns * 2, transcendentals=0
        ),
        name="ladder",
    )(packed, pair_values)
    partial_sums = lax.all_to_all(partial_sums, "cd", split_axis=0, concat_axis=0, tiled=True)
    return jnp.sum(partial_sums.astype(jnp.float32), axis=0).astype(jnp.bfloat16)


def solution(mesh):
    placed = (P("ab", "cd"), P("ab", "cd", None), P("cd"), P("cd"), P("cd"))
    return jax.shard_map(
        on_device, mesh=mesh, in_specs=placed, out_specs=P(None, ("ab", "cd")), check_vma=False
    )
```

```python
import functools

import jax
import jax.numpy as jnp
from jax import lax
from jax.experimental import pallas as pl
from jax.experimental.pallas import tpu as pltpu
from jax.sharding import PartitionSpec as P

LANES = 128
DEPTH = 512
MIB = 1024 * 1024
VMEM = pl.BlockSpec(memory_space=pltpu.VMEM)


def group_size(orbits):
    return max(g for g in range(1, orbits + 1) if orbits % g == 0 and g * orbits <= DEPTH)


def params(mib):
    return pltpu.CompilerParams(vmem_limit_bytes=mib * MIB)


def cost(flops, bytes_accessed):
    return pl.CostEstimate(flops=flops, bytes_accessed=bytes_accessed, transcendentals=0)


def code_kernel(slabs, orbits, shift, first_ref, second_ref, coded_ref):
    base = lax.axis_index("cd") * orbits
    coded = ((first_ref[...] - base) << shift) + second_ref[...]
    for s in range(slabs):
        coded_ref[s] = coded


def pack_kernel(slabs, orbits, group, pairs, table_ref, packed_ref):
    for s in range(slabs):
        for g in range(table_ref.shape[0] // (group * pairs)):
            parts = [
                table_ref[(g * group + k) * pairs : (g * group + k + 1) * pairs, s * orbits : (s + 1) * orbits]
                for k in range(group)
            ]
            if group * orbits < DEPTH:
                parts.append(jnp.zeros((pairs, DEPTH - group * orbits), jnp.bfloat16))
            packed_ref[s, g * pairs : (g + 1) * pairs, :] = jnp.concatenate(parts, axis=1)


def lookup(table, pairs, keys, groups, totals):
    per_row = keys.shape[0]
    width = per_row * LANES
    key = jnp.concatenate([keys[j : j + 1] for j in range(per_row)], axis=1)
    chosen = jnp.concatenate([groups[j : j + 1] for j in range(per_row)], axis=1)
    hot = jnp.where(lax.broadcasted_iota(jnp.int32, (DEPTH, width), 0) == key, 1.0, 0.0).astype(jnp.bfloat16)
    sums = jnp.dot(table, hot, preferred_element_type=jnp.float32)
    chosen = jnp.broadcast_to(chosen, (8, width))
    totals = list(totals)
    for g in range(table.shape[0] // pairs):
        mine = chosen == g
        for t in range(pairs // 8):
            at = g * pairs + t * 8
            totals[t] = jnp.where(mine, sums[at : at + 8], totals[t])
    return totals


def crossed_kernel(slabs, orbits, group, pairs, shift, packed_ref, coded_ref, crossed_ref):
    base = lax.axis_index("cd") * orbits
    lines = coded_ref.shape[1]
    for s in range(slabs):
        coded = coded_ref[s]
        first = coded >> shift
        second = (coded & ((1 << shift) - 1)) - base
        here = jnp.logical_and(second >= 0, second < orbits)
        second = jnp.where(here, second, 0)
        groups = lax.div(second, jnp.int32(group))
        keys = (second - groups * group) * orbits + first
        groups = jnp.where(here, groups, -1)
        step = min(lines, 4)
        for i in range(0, lines, step):
            zero = [jnp.zeros((8, step * LANES), jnp.float32)] * (pairs // 8)
            got = lookup(packed_ref[s], pairs, keys[i : i + step], groups[i : i + step], zero)
            crossed_ref[s, :, i * LANES : (i + step) * LANES] = jnp.concatenate(got, axis=0).astype(jnp.bfloat16)


def direct_kernel(slabs, orbits, group, pairs, shift, packed_ref, coded_ref, direct_ref):
    coded = coded_ref[lax.axis_index("cd")]
    first = coded >> shift
    second = coded & ((1 << shift) - 1)
    groups = lax.div(first, jnp.int32(group))
    owner = lax.div(second, jnp.int32(orbits))
    keys = (first - groups * group) * orbits + (second - owner * orbits)
    lines = coded.shape[0]
    step = min(lines, 4)
    for i in range(0, lines, step):
        got = [jnp.zeros((8, step * LANES), jnp.float32)] * (pairs // 8)
        for s in range(slabs):
            chosen = jnp.where(owner[i : i + step] == s, groups[i : i + step], -1)
            got = lookup(packed_ref[s], pairs, keys[i : i + step], chosen, got)
        direct_ref[:, i * LANES : (i + step) * LANES] = jnp.concatenate(got, axis=0).astype(jnp.bfloat16)


def ladder_kernel(packed_ref, values_ref, out_ref):
    slabs, _, width = out_ref.shape
    for s in range(slabs):
        out_ref[s] = lax.dot_general(
            values_ref[s * width : (s + 1) * width, :],
            packed_ref[...],
            (((1,), (1,)), ((), ())),
            preferred_element_type=jnp.float32,
        ).T.astype(jnp.bfloat16)


def on_device(pair_values, amplitudes, cd_first, cd_second, live_cols):
    slabs = lax.axis_size("cd")
    blocks = lax.axis_size("ab")
    pair_block, orbits, orbitals = amplitudes.shape
    columns = cd_first.shape[0]
    rows = pair_values.shape[0]
    lines = columns // LANES
    pairs = -(-pair_block // 16) * 16
    group = group_size(orbits)
    shift = (orbitals - 1).bit_length()

    coded = pl.pallas_call(
        functools.partial(code_kernel, slabs, orbits, shift),
        out_shape=jax.ShapeDtypeStruct((slabs, lines, LANES), jnp.int32),
        in_specs=[VMEM] * 2,
        out_specs=VMEM,
        compiler_params=params(4),
        cost_estimate=cost(slabs * columns, slabs * columns * 4),
        name="code",
    )(cd_first.reshape(lines, LANES), cd_second.reshape(lines, LANES))
    coded = lax.all_to_all(coded, "cd", split_axis=0, concat_axis=0, tiled=True)

    table = jnp.transpose(amplitudes, (1, 0, 2))
    if pairs != pair_block:
        table = jnp.pad(table, ((0, 0), (0, pairs - pair_block), (0, 0)))
    table = table.reshape(orbits * pairs, orbitals)
    packed_rows = orbits // group * pairs
    steps = 4 if orbits // group % 4 == 0 else 1
    table = pl.pallas_call(
        functools.partial(pack_kernel, slabs, orbits, group, pairs),
        out_shape=jax.ShapeDtypeStruct((slabs, packed_rows, DEPTH), jnp.bfloat16),
        grid=(steps,),
        in_specs=[pl.BlockSpec((orbits * pairs // steps, orbitals), lambda i: (i, 0))],
        out_specs=pl.BlockSpec((slabs, packed_rows // steps, DEPTH), lambda i: (0, i, 0)),
        compiler_params=params(16),
        cost_estimate=cost(0, 4 * orbits * pairs * orbitals),
        name="pack",
    )(table)

    lookup_flops = 2 * slabs * packed_rows * DEPTH * columns
    lookup_bytes = slabs * packed_rows * DEPTH * 2 + slabs * columns * pairs * 2
    crossed = pl.pallas_call(
        functools.partial(crossed_kernel, slabs, orbits, group, pairs, shift),
        out_shape=jax.ShapeDtypeStruct((slabs, pairs, columns), jnp.bfloat16),
        in_specs=[VMEM] * 2,
        out_specs=VMEM,
        compiler_params=params(20),
        cost_estimate=cost(lookup_flops, lookup_bytes),
        name="crossed",
    )(table, coded)
    crossed = lax.all_to_all(crossed, "cd", split_axis=0, concat_axis=0, tiled=True)
    direct = pl.pallas_call(
        functools.partial(direct_kernel, slabs, orbits, group, pairs, shift),
        out_shape=jax.ShapeDtypeStruct((pairs, columns), jnp.bfloat16),
        in_specs=[VMEM] * 2,
        out_specs=VMEM,
        compiler_params=params(20),
        cost_estimate=cost(lookup_flops, lookup_bytes),
        name="direct",
    )(table, coded)
    crossed = jnp.sum(crossed.astype(jnp.float32), axis=0)

    slots = jnp.arange(columns, dtype=jnp.int32)
    live = (slots < live_cols[0]).astype(jnp.float32)
    half = jnp.where(cd_first == cd_second, jnp.float32(0.5), jnp.float32(1.0))
    packed = ((direct.astype(jnp.float32) + crossed) * (half * live)[None, :]).astype(jnp.bfloat16)
    packed = lax.all_gather(packed[:pair_block], "ab", axis=0, tiled=True)

    width = rows // slabs
    partial_sums = pl.pallas_call(
        ladder_kernel,
        out_shape=jax.ShapeDtypeStruct((slabs, blocks * pair_block, width), jnp.bfloat16),
        in_specs=[VMEM] * 2,
        out_specs=VMEM,
        compiler_params=params(20),
        cost_estimate=cost(2 * blocks * pair_block * columns * rows, rows * columns * 2),
        name="ladder",
    )(packed, pair_values)
    partial_sums = lax.all_to_all(partial_sums, "cd", split_axis=0, concat_axis=0, tiled=True)
    return jnp.sum(partial_sums.astype(jnp.float32), axis=0).astype(jnp.bfloat16)


def solution(mesh):
    placed = (P("ab", "cd"), P("ab", "cd", None), P("cd"), P("cd"), P("cd"))
    return jax.shard_map(
        on_device, mesh=mesh, in_specs=placed, out_specs=P(None, ("ab", "cd")), check_vma=False
    )
```

```python
import functools

import jax
import jax.numpy as jnp
from jax import lax
from jax.experimental import pallas as pl
from jax.experimental.pallas import tpu as pltpu
from jax.sharding import PartitionSpec as P

LANES = 128
DEPTH = 512
MIB = 1024 * 1024
VMEM = pl.BlockSpec(memory_space=pltpu.VMEM)
ANY = pl.BlockSpec(memory_space=pl.ANY)


def group_size(orbits):
    return max(g for g in range(1, orbits + 1) if orbits % g == 0 and g * orbits <= DEPTH)


def params(mib):
    return pltpu.CompilerParams(vmem_limit_bytes=mib * MIB)


def cost(flops, bytes_accessed):
    return pl.CostEstimate(flops=flops, bytes_accessed=bytes_accessed, transcendentals=0)


SMALL = cost(1, 1)


def swap(x, axis, size, mask):
    return lax.ppermute(x, axis, [(i, i ^ mask) for i in range(size)])


def code_kernel(slabs, orbits, shift, first_ref, second_ref, coded_ref, first_here, second_here, sems):
    copies = [
        pltpu.make_async_copy(first_ref, first_here, sems.at[0]),
        pltpu.make_async_copy(second_ref, second_here, sems.at[1]),
    ]
    for copy in copies:
        copy.start()
    for copy in copies:
        copy.wait()
    base = lax.axis_index("cd") * orbits
    coded = ((first_here[...] - base) << shift) + second_here[...]
    for s in range(slabs):
        coded_ref[s] = coded


def pack_kernel(slabs, orbits, group, pairs, table_ref, packed_ref):
    for s in range(slabs):
        for g in range(table_ref.shape[0] // (group * pairs)):
            parts = [
                table_ref[(g * group + k) * pairs : (g * group + k + 1) * pairs, s * orbits : (s + 1) * orbits]
                for k in range(group)
            ]
            if group * orbits < DEPTH:
                parts.append(jnp.zeros((pairs, DEPTH - group * orbits), jnp.bfloat16))
            packed_ref[s, g * pairs : (g + 1) * pairs, :] = jnp.concatenate(parts, axis=1)


def lookup(table, pairs, keys, groups, totals):
    per_row = keys.shape[0]
    width = per_row * LANES
    key = jnp.concatenate([keys[j : j + 1] for j in range(per_row)], axis=1)
    chosen = jnp.concatenate([groups[j : j + 1] for j in range(per_row)], axis=1)
    hot = jnp.where(lax.broadcasted_iota(jnp.int32, (DEPTH, width), 0) == key, 1.0, 0.0).astype(jnp.bfloat16)
    sums = jnp.dot(table, hot, preferred_element_type=jnp.float32)
    chosen = jnp.broadcast_to(chosen, (8, width))
    totals = list(totals)
    for g in range(table.shape[0] // pairs):
        mine = chosen == g
        for t in range(pairs // 8):
            at = g * pairs + t * 8
            totals[t] = jnp.where(mine, sums[at : at + 8], totals[t])
    return totals


def crossed_blocks(group, pairs, shift, orbits, masks, packed_ref, coded_ref, crossed_ref):
    me = lax.axis_index("cd")
    base = me * orbits
    lines = coded_ref.shape[1]
    step = min(lines, 4)

    def block(out, mask):
        slab = me ^ mask
        coded = coded_ref[slab]
        first = coded >> shift
        second = (coded & ((1 << shift) - 1)) - base
        here = jnp.logical_and(second >= 0, second < orbits)
        second = jnp.where(here, second, 0)
        groups = lax.div(second, jnp.int32(group))
        keys = (second - groups * group) * orbits + first
        groups = jnp.where(here, groups, -1)
        for i in range(0, lines, step):
            zero = [jnp.zeros((8, step * LANES), jnp.float32)] * (pairs // 8)
            got = lookup(packed_ref[slab], pairs, keys[i : i + step], groups[i : i + step], zero)
            crossed_ref[out, :, i * LANES : (i + step) * LANES] = jnp.concatenate(got, axis=0).astype(jnp.bfloat16)

    for at in range(0, len(masks), 2):
        some = list(range(at, min(at + 2, len(masks))))
        needed = functools.reduce(jnp.logical_or, [(me ^ masks[out]) <= me for out in some])

        @pl.when(needed)
        def _(some=some):
            for out in some:
                block(out, masks[out])

        @pl.when(jnp.logical_not(needed))
        def _(some=some):
            for out in some:
                crossed_ref[out] = jnp.zeros(crossed_ref.shape[1:], jnp.bfloat16)


def direct_kernel(group, pairs, shift, orbits, slabs, low, high, packed_ref, coded_ref, *refs):
    old_ref, direct_ref = refs[0], refs[-1]
    me = lax.axis_index("cd")
    coded = coded_ref[0]
    first = coded >> shift
    second = coded & ((1 << shift) - 1)
    groups = lax.div(first, jnp.int32(group))
    owner = lax.div(second, jnp.int32(orbits))
    keys = (first - groups * group) * orbits + (second - owner * orbits)
    lines = coded.shape[0]
    step = min(lines, 4)
    direct_ref[...] = jnp.zeros(direct_ref.shape, jnp.bfloat16) if old_ref is None else old_ref[...]

    for ahead in range(low, high):

        @pl.when(me + ahead < slabs)
        def _(ahead=ahead):
            slab = me + ahead
            for i in range(0, lines, step):
                here = slice(i * LANES, (i + step) * LANES)
                old = direct_ref[:, here].astype(jnp.float32)
                got = [old[t * 8 : (t + 1) * 8] for t in range(pairs // 8)]
                chosen = jnp.where(owner[i : i + step] == slab, groups[i : i + step], -1)
                got = lookup(packed_ref[slab], pairs, keys[i : i + step], chosen, got)
                direct_ref[:, here] = jnp.concatenate(got, axis=0).astype(jnp.bfloat16)


def direct_first(*args):
    *head, direct_ref = args
    direct_kernel(*head, None, direct_ref)


def crossed_kernel(group, pairs, shift, orbits, masks, packed_ref, coded_ref, *refs):
    crossed_ref = refs[-1]
    crossed_blocks(group, pairs, shift, orbits, masks, packed_ref, coded_ref, crossed_ref)


def ladder_kernel(masks, parts, *refs):
    packed_refs, values_ref, out_ref = refs[:parts], refs[parts], refs[-1]
    width = out_ref.shape[2]
    me = lax.axis_index("cd")
    packed = jnp.concatenate([ref[...] for ref in packed_refs], axis=0)
    for out, mask in enumerate(masks):
        at = pl.ds(pl.multiple_of((me ^ mask) * width, width), width)
        out_ref[out] = lax.dot_general(
            values_ref[at, :],
            packed,
            (((1,), (1,)), ((), ())),
            preferred_element_type=jnp.float32,
        ).T.astype(out_ref.dtype)


def on_device(pair_values, amplitudes, cd_first, cd_second, live_cols):
    slabs = lax.axis_size("cd")
    blocks = lax.axis_size("ab")
    pair_block, orbits, orbitals = amplitudes.shape
    columns = cd_first.shape[0]
    rows = pair_values.shape[0]
    lines = columns // LANES
    pairs = -(-pair_block // 16) * 16
    group = group_size(orbits)
    shift = (orbitals - 1).bit_length()
    near = list(range(0, slabs, 2))
    far = list(range(1, slabs, 2))

    coded = pl.pallas_call(
        functools.partial(code_kernel, slabs, orbits, shift),
        out_shape=jax.ShapeDtypeStruct((slabs, lines, LANES), jnp.int32),
        in_specs=[ANY] * 2,
        out_specs=VMEM,
        scratch_shapes=[pltpu.VMEM((lines, LANES), jnp.int32)] * 2 + [pltpu.SemaphoreType.DMA((2,))],
        compiler_params=params(58),
        cost_estimate=cost(slabs * columns, slabs * columns * 4),
        name="code",
    )(cd_first.reshape(lines, LANES), cd_second.reshape(lines, LANES))
    own_coded = coded
    coded = lax.all_to_all(coded, "cd", split_axis=0, concat_axis=0, tiled=True)

    table = jnp.transpose(amplitudes, (1, 0, 2))
    if pairs != pair_block:
        table = jnp.pad(table, ((0, 0), (0, pairs - pair_block), (0, 0)))
    table = table.reshape(orbits * pairs, orbitals)
    packed_rows = orbits // group * pairs
    steps = 4 if orbits // group % 4 == 0 else 1
    table = pl.pallas_call(
        functools.partial(pack_kernel, slabs, orbits, group, pairs),
        out_shape=jax.ShapeDtypeStruct((slabs, packed_rows, DEPTH), jnp.bfloat16),
        grid=(steps,),
        in_specs=[pl.BlockSpec((orbits * pairs // steps, orbitals), lambda i: (i, 0))],
        out_specs=pl.BlockSpec((slabs, packed_rows // steps, DEPTH), lambda i: (0, i, 0)),
        compiler_params=params(16),
        cost_estimate=cost(0, 4 * orbits * pairs * orbitals),
        name="pack",
    )(table)

    lookup_flops = 2 * packed_rows * DEPTH * columns
    lookup_bytes = packed_rows * DEPTH * 2 + columns * pairs * 2

    def direct_for(low, high, *old):
        return pl.pallas_call(
            functools.partial(direct_kernel if old else direct_first, group, pairs, shift, orbits, slabs, low, high),
            out_shape=jax.ShapeDtypeStruct((pairs, columns), jnp.bfloat16),
            in_specs=[VMEM] * 2 + [VMEM, ANY][: len(old)],
            out_specs=VMEM,
            compiler_params=params(20),
            cost_estimate=cost((high - low) * lookup_flops, (high - low) * lookup_bytes),
            name="direct",
        )(table, own_coded, *old)

    direct = direct_for(0, slabs // 2)
    coded, direct = lax.optimization_barrier((coded, direct))

    def crossed_for(masks, name, *after):
        return pl.pallas_call(
            functools.partial(crossed_kernel, group, pairs, shift, orbits, masks),
            out_shape=jax.ShapeDtypeStruct((len(masks), pairs, columns), jnp.bfloat16),
            in_specs=[VMEM] * 2 + [ANY] * len(after),
            out_specs=VMEM,
            compiler_params=params(20),
            cost_estimate=cost(len(masks) * lookup_flops, len(masks) * lookup_bytes),
            name=name,
        )(table, coded, *after)

    arrived, last = [], ()
    for at in reversed(range(0, len(far), 2)):
        last = (crossed_for(far[at : at + 2], "crossed_far", *last),)
        arrived.insert(0, swap(last[0], "cd", slabs, 1))
    crossed = crossed_for(near, "crossed_near", *last)
    direct = direct_for(slabs // 2, slabs, direct, crossed)
    merged = [crossed[k] + arrived[k // 2][k % 2] for k in range(len(near))]
    got = [swap(merged[k], "cd", slabs, near[k]) for k in reversed(range(1, len(near)))]
    crossed = merged[0].astype(jnp.float32)
    for block in got:
        crossed = crossed + block.astype(jnp.float32)

    slots = jnp.arange(columns, dtype=jnp.int32)
    live = (slots < live_cols[0]).astype(jnp.float32)
    half = jnp.where(cd_first == cd_second, jnp.float32(0.5), jnp.float32(1.0))
    packed = ((direct.astype(jnp.float32) + crossed) * (half * live)[None, :]).astype(jnp.bfloat16)

    gathered = [lax.all_gather(packed[:pair_block], "ab", axis=0, tiled=True)]
    all_pairs = blocks * pair_block

    width = rows // slabs

    def ladder_for(masks, dtype, name, *after):
        return pl.pallas_call(
            functools.partial(ladder_kernel, masks, len(gathered)),
            out_shape=jax.ShapeDtypeStruct((len(masks), all_pairs, width), dtype),
            in_specs=[VMEM] * (len(gathered) + 1) + [ANY] * len(after),
            out_specs=VMEM,
            compiler_params=params(16),
            cost_estimate=SMALL,
            name=name,
        )(*gathered, pair_values, *after)

    got, last = [], ()
    for mask in reversed(near[1:]):
        last = (ladder_for([mask, mask + 1], jnp.bfloat16, "ladder", *last),)
        got.append(swap(last[0], "cd", slabs, mask))
    total = ladder_for([0, 1], jnp.float32, "ladder_own", *last)
    for part in got:
        total = total + part.astype(jnp.float32)
    total = total[0] + swap(total[1].astype(jnp.bfloat16), "cd", slabs, 1).astype(jnp.float32)
    return total.astype(jnp.bfloat16)


def solution(mesh):
    placed = (P("ab", "cd"), P("ab", "cd", None), P("cd"), P("cd"), P("cd"))
    return jax.shard_map(
        on_device, mesh=mesh, in_specs=placed, out_specs=P(None, ("ab", "cd")), check_vma=False
    )
```

```python
import functools

import jax
import jax.numpy as jnp
from jax import lax
from jax.experimental import pallas as pl
from jax.experimental.pallas import tpu as pltpu
from jax.sharding import PartitionSpec as P

LANES = 128
DEPTH = 512
MIB = 1024 * 1024
VMEM = pl.BlockSpec(memory_space=pltpu.VMEM)
ANY = pl.BlockSpec(memory_space=pl.ANY)


def group_size(orbits):
    return max(g for g in range(1, orbits + 1) if orbits % g == 0 and g * orbits <= DEPTH)


def params(mib):
    return pltpu.CompilerParams(vmem_limit_bytes=mib * MIB)


def cost(flops, bytes_accessed):
    return pl.CostEstimate(flops=flops, bytes_accessed=bytes_accessed, transcendentals=0)


def spent(microseconds):
    return cost(int(microseconds * 1.1e9), 1)


SMALL = spent(0.01)


def swap(x, axis, size, mask):
    return lax.ppermute(x, axis, [(i, i ^ mask) for i in range(size)])


def code_kernel(slabs, orbits, shift, first_ref, second_ref, live_ref, coded_ref, first_here, second_here, live_here, sems):
    copies = [
        pltpu.make_async_copy(first_ref, first_here, sems.at[0]),
        pltpu.make_async_copy(second_ref, second_here, sems.at[1]),
        pltpu.make_async_copy(live_ref, live_here, sems.at[2]),
    ]
    for copy in copies:
        copy.start()
    for copy in copies:
        copy.wait()
    base = lax.axis_index("cd") * orbits
    coded = ((first_here[...] - base) << shift) + second_here[...]
    shape = coded.shape
    slots = lax.broadcasted_iota(jnp.int32, shape, 0) * shape[1] + lax.broadcasted_iota(jnp.int32, shape, 1)
    coded = jnp.where(slots < live_here[0], coded, -1)
    for s in range(slabs):
        coded_ref[s] = coded


def pack_kernel(slabs, orbits, group, pairs, table_ref, packed_ref):
    for s in range(slabs):
        for g in range(table_ref.shape[0] // (group * pairs)):
            parts = [
                table_ref[(g * group + k) * pairs : (g * group + k + 1) * pairs, s * orbits : (s + 1) * orbits]
                for k in range(group)
            ]
            if group * orbits < DEPTH:
                parts.append(jnp.zeros((pairs, DEPTH - group * orbits), jnp.bfloat16))
            packed_ref[s, g * pairs : (g + 1) * pairs, :] = jnp.concatenate(parts, axis=1)


def lookup(table, pairs, keys, groups, totals):
    per_row = keys.shape[0]
    width = per_row * LANES
    key = jnp.concatenate([keys[j : j + 1] for j in range(per_row)], axis=1)
    chosen = jnp.concatenate([groups[j : j + 1] for j in range(per_row)], axis=1)
    hot = jnp.where(lax.broadcasted_iota(jnp.int32, (DEPTH, width), 0) == key, 1.0, 0.0).astype(jnp.bfloat16)
    sums = jnp.dot(table, hot, preferred_element_type=jnp.float32)
    chosen = jnp.broadcast_to(chosen, (8, width))
    totals = list(totals)
    for g in range(table.shape[0] // pairs):
        mine = chosen == g
        for t in range(pairs // 8):
            at = g * pairs + t * 8
            totals[t] = jnp.where(mine, sums[at : at + 8], totals[t])
    return totals


def crossed_blocks(group, pairs, shift, orbits, masks, packed_ref, coded_ref, crossed_ref):
    me = lax.axis_index("cd")
    base = me * orbits
    lines = coded_ref.shape[1]
    step = min(lines, 4)

    def block(out, mask):
        slab = me ^ mask
        coded = coded_ref[slab]
        first = coded >> shift
        second = (coded & ((1 << shift) - 1)) - base
        here = jnp.logical_and(coded >= 0, jnp.logical_and(second >= 0, second < orbits))
        second = jnp.where(here, second, 0)
        groups = lax.div(second, jnp.int32(group))
        keys = (second - groups * group) * orbits + first
        groups = jnp.where(here, groups, -1)
        for i in range(0, lines, step):
            zero = [jnp.zeros((8, step * LANES), jnp.float32)] * (pairs // 8)
            got = lookup(packed_ref[slab], pairs, keys[i : i + step], groups[i : i + step], zero)
            crossed_ref[out, :, i * LANES : (i + step) * LANES] = jnp.concatenate(got, axis=0).astype(jnp.bfloat16)

    for at in range(0, len(masks), 2):
        some = list(range(at, min(at + 2, len(masks))))
        needed = functools.reduce(jnp.logical_or, [(me ^ masks[out]) <= me for out in some])

        @pl.when(needed)
        def _(some=some):
            for out in some:
                block(out, masks[out])

        @pl.when(jnp.logical_not(needed))
        def _(some=some):
            for out in some:
                crossed_ref[out] = jnp.zeros(crossed_ref.shape[1:], jnp.bfloat16)


def direct_kernel(group, pairs, shift, orbits, slabs, low, high, packed_ref, coded_ref, *refs):
    old_ref, direct_ref = refs[0], refs[-1]
    me = lax.axis_index("cd")
    coded = coded_ref[0]
    first = coded >> shift
    second = coded & ((1 << shift) - 1)
    groups = jnp.where(coded >= 0, lax.div(first, jnp.int32(group)), -1)
    owner = lax.div(second, jnp.int32(orbits))
    keys = lax.rem(first, jnp.int32(group)) * orbits + (second - owner * orbits)
    lines = coded.shape[0]
    step = min(lines, 4)
    direct_ref[...] = jnp.zeros(direct_ref.shape, jnp.bfloat16) if old_ref is None else old_ref[...]

    for ahead in range(low, high):

        @pl.when(me + ahead < slabs)
        def _(ahead=ahead):
            slab = me + ahead
            for i in range(0, lines, step):
                here = slice(i * LANES, (i + step) * LANES)
                old = direct_ref[:, here].astype(jnp.float32)
                got = [old[t * 8 : (t + 1) * 8] for t in range(pairs // 8)]
                chosen = jnp.where(owner[i : i + step] == slab, groups[i : i + step], -1)
                got = lookup(packed_ref[slab], pairs, keys[i : i + step], chosen, got)
                direct_ref[:, here] = jnp.concatenate(got, axis=0).astype(jnp.bfloat16)


def direct_first(*args):
    *head, direct_ref = args
    direct_kernel(*head, None, direct_ref)


def crossed_kernel(group, pairs, shift, orbits, masks, packed_ref, coded_ref, *refs):
    crossed_ref = refs[-1]
    crossed_blocks(group, pairs, shift, orbits, masks, packed_ref, coded_ref, crossed_ref)


def ladder_kernel(masks, parts, *refs):
    packed_refs, values_ref, out_ref = refs[:parts], refs[parts], refs[-1]
    width = out_ref.shape[2]
    me = lax.axis_index("cd")
    packed = jnp.concatenate([ref[...] for ref in packed_refs], axis=0)
    for out, mask in enumerate(masks):
        at = pl.ds(pl.multiple_of((me ^ mask) * width, width), width)
        out_ref[out] = lax.dot_general(
            values_ref[at, :],
            packed,
            (((1,), (1,)), ((), ())),
            preferred_element_type=jnp.float32,
        ).T.astype(out_ref.dtype)


def add_kernel(*refs):
    total = refs[0][...]
    for ref in refs[1:-1]:
        total = total + ref[...].astype(jnp.float32)
    refs[-1][...] = total


def add_up(total, parts):
    for part in parts[:-1]:
        total = pl.pallas_call(
            add_kernel,
            out_shape=jax.ShapeDtypeStruct(total.shape, total.dtype),
            in_specs=[VMEM] * 2,
            out_specs=VMEM,
            compiler_params=params(8),
            cost_estimate=spent(0.5),
            name="add",
        )(total, part)
    return total + parts[-1].astype(jnp.float32)


def on_device(pair_values, amplitudes, cd_first, cd_second, live_cols):
    slabs = lax.axis_size("cd")
    blocks = lax.axis_size("ab")
    pair_block, orbits, orbitals = amplitudes.shape
    columns = cd_first.shape[0]
    rows = pair_values.shape[0]
    lines = columns // LANES
    pairs = -(-pair_block // 16) * 16
    group = group_size(orbits)
    shift = (orbitals - 1).bit_length()
    near = list(range(0, slabs, 2))
    far = list(range(1, slabs, 2))

    coded = pl.pallas_call(
        functools.partial(code_kernel, slabs, orbits, shift),
        out_shape=jax.ShapeDtypeStruct((slabs, lines, LANES), jnp.int32),
        in_specs=[ANY] * 3,
        out_specs=VMEM,
        scratch_shapes=[pltpu.VMEM((lines, LANES), jnp.int32)] * 2
        + [pltpu.SMEM((1,), jnp.int32), pltpu.SemaphoreType.DMA((3,))],
        compiler_params=params(58),
        cost_estimate=spent(20),
        name="code",
    )(cd_first.reshape(lines, LANES), cd_second.reshape(lines, LANES), live_cols)
    own_coded = coded
    coded = lax.all_to_all(coded, "cd", split_axis=0, concat_axis=0, tiled=True)

    table = jnp.transpose(amplitudes, (1, 0, 2))
    if pairs != pair_block:
        table = jnp.pad(table, ((0, 0), (0, pairs - pair_block), (0, 0)))
    table = table.reshape(orbits * pairs, orbitals)
    packed_rows = orbits // group * pairs
    steps = 4 if orbits // group % 4 == 0 else 1
    table = pl.pallas_call(
        functools.partial(pack_kernel, slabs, orbits, group, pairs),
        out_shape=jax.ShapeDtypeStruct((slabs, packed_rows, DEPTH), jnp.bfloat16),
        grid=(steps,),
        in_specs=[pl.BlockSpec((orbits * pairs // steps, orbitals), lambda i: (i, 0))],
        out_specs=pl.BlockSpec((slabs, packed_rows // steps, DEPTH), lambda i: (0, i, 0)),
        compiler_params=params(16),
        cost_estimate=cost(0, 4 * orbits * pairs * orbitals),
        name="pack",
    )(table)

    lookup_flops = 2 * packed_rows * DEPTH * columns
    lookup_bytes = packed_rows * DEPTH * 2 + columns * pairs * 2

    def direct_for(low, high, *old):
        return pl.pallas_call(
            functools.partial(direct_kernel if old else direct_first, group, pairs, shift, orbits, slabs, low, high),
            out_shape=jax.ShapeDtypeStruct((pairs, columns), jnp.bfloat16),
            in_specs=[VMEM] * 2 + [VMEM, ANY][: len(old)],
            out_specs=VMEM,
            compiler_params=params(20),
            cost_estimate=SMALL if old else cost((high - low) * lookup_flops, 1),
            name="direct",
        )(table, own_coded, *old)

    cuts = sorted({0, min(2, slabs), min(4, slabs), slabs})
    direct = direct_for(cuts[0], cuts[1])
    coded, direct = lax.optimization_barrier((coded, direct))

    def crossed_for(masks, name, *after):
        return pl.pallas_call(
            functools.partial(crossed_kernel, group, pairs, shift, orbits, masks),
            out_shape=jax.ShapeDtypeStruct((len(masks), pairs, columns), jnp.bfloat16),
            in_specs=[VMEM] * 2 + [ANY] * len(after),
            out_specs=VMEM,
            compiler_params=params(20),
            cost_estimate=SMALL,
            name=name,
        )(table, coded, *after)

    pairs_of = [near[at : at + 2] for at in reversed(range(0, slabs // 2, 2))]
    arrived, last = [], ()
    for masks in pairs_of:
        last = (crossed_for([mask + 1 for mask in masks], "crossed_far", *last),)
        arrived.append(swap(last[0], "cd", slabs, 1))
    got = []
    for masks, block in zip(pairs_of, arrived):
        merged = crossed_for(masks, "crossed_near", *last) + block
        last = (merged,)
        for k in reversed(range(len(masks))):
            if masks[k]:
                got.append(swap(merged[k], "cd", slabs, masks[k]))
    for low, high in zip(cuts[1:], cuts[2:]):
        direct = direct_for(low, high, direct, *last)
    crossed = add_up(merged[0].astype(jnp.float32), got)
    half = jnp.where(cd_first == cd_second, jnp.float32(0.5), jnp.float32(1.0))
    packed = ((direct.astype(jnp.float32) + crossed) * half[None, :]).astype(jnp.bfloat16)

    gathered = [lax.all_gather(packed[:pair_block], "ab", axis=0, tiled=True)]
    all_pairs = blocks * pair_block

    width = rows // slabs

    def ladder_for(masks, dtype, name, *after):
        return pl.pallas_call(
            functools.partial(ladder_kernel, masks, len(gathered)),
            out_shape=jax.ShapeDtypeStruct((len(masks), all_pairs, width), dtype),
            in_specs=[VMEM] * (len(gathered) + 1) + [ANY] * len(after),
            out_specs=VMEM,
            compiler_params=params(16),
            cost_estimate=SMALL,
            name=name,
        )(*gathered, pair_values, *after)

    got, last = [], ()
    for mask in reversed(near[1:]):
        last = (ladder_for([mask, mask + 1], jnp.bfloat16, "ladder", *last),)
        got.append(swap(last[0], "cd", slabs, mask))
    total = ladder_for([0, 1], jnp.float32, "ladder_own", *last)
    total = add_up(total, got)
    total = total[0] + swap(total[1].astype(jnp.bfloat16), "cd", slabs, 1).astype(jnp.float32)
    return total.astype(jnp.bfloat16)


def solution(mesh):
    placed = (P("ab", "cd"), P("ab", "cd", None), P("cd"), P("cd"), P("cd"))
    return jax.shard_map(
        on_device, mesh=mesh, in_specs=placed, out_specs=P(None, ("ab", "cd")), check_vma=False
    )
```

```python
import functools

import jax
import jax.numpy as jnp
from jax import lax
from jax.experimental import pallas as pl
from jax.experimental.pallas import tpu as pltpu
from jax.sharding import PartitionSpec as P

LANES = 128
DEPTH = 512
MIB = 1024 * 1024
VMEM = pl.BlockSpec(memory_space=pltpu.VMEM)
ANY = pl.BlockSpec(memory_space=pl.ANY)
HBM = pl.BlockSpec(memory_space=pltpu.HBM)


def group_size(orbits):
    return max(g for g in range(1, orbits + 1) if orbits % g == 0 and g * orbits <= DEPTH)


def params(mib):
    return pltpu.CompilerParams(vmem_limit_bytes=mib * MIB)


def cost(flops, bytes_accessed):
    return pl.CostEstimate(flops=flops, bytes_accessed=bytes_accessed, transcendentals=0)


def spent(microseconds):
    return cost(int(microseconds * 1.1e9), 1)


SMALL = spent(0.01)


def in_hbm(x):
    return pltpu.with_memory_space_constraint(x, pltpu.HBM)


def swap(x, axis, size, mask):
    return lax.ppermute(x, axis, [(i, i ^ mask) for i in range(size)])


def code_kernel(slabs, orbits, shift, first_ref, second_ref, coded_ref, own_ref, first_here, second_here, sems):
    copies = [
        pltpu.make_async_copy(first_ref, first_here, sems.at[0]),
        pltpu.make_async_copy(second_ref, second_here, sems.at[1]),
    ]
    for copy in copies:
        copy.start()
    for copy in copies:
        copy.wait()
    base = lax.axis_index("cd") * orbits
    coded = ((first_here[...] - base) << shift) + second_here[...]
    own_ref[...] = coded
    for s in range(slabs):
        coded_ref[s] = coded


def pack_kernel(slabs, orbits, group, pairs, table_ref, packed_ref, here_ref, sems):
    steps = sems.shape[0]
    rows = table_ref.shape[0] // steps
    copies = []
    for i in range(steps):
        at = pl.ds(i * rows, rows)
        copies.append(pltpu.make_async_copy(table_ref.at[at], here_ref.at[at], sems.at[i]))
        copies[i].start()
    per_step = rows // (group * pairs)
    for i in range(steps):
        copies[i].wait()
        for s in range(slabs):
            for g in range(i * per_step, (i + 1) * per_step):
                parts = [
                    here_ref[(g * group + k) * pairs : (g * group + k + 1) * pairs, s * orbits : (s + 1) * orbits]
                    for k in range(group)
                ]
                if group * orbits < DEPTH:
                    parts.append(jnp.zeros((pairs, DEPTH - group * orbits), jnp.bfloat16))
                packed_ref[s, g * pairs : (g + 1) * pairs, :] = jnp.concatenate(parts, axis=1)


def lookup(table, pairs, keys, groups, totals):
    per_row = keys.shape[0]
    width = per_row * LANES
    key = jnp.concatenate([keys[j : j + 1] for j in range(per_row)], axis=1)
    chosen = jnp.concatenate([groups[j : j + 1] for j in range(per_row)], axis=1)
    hot = jnp.where(lax.broadcasted_iota(jnp.int32, (DEPTH, width), 0) == key, 1.0, 0.0).astype(jnp.bfloat16)
    sums = jnp.dot(table, hot, preferred_element_type=jnp.float32)
    chosen = jnp.broadcast_to(chosen, (8, width))
    totals = list(totals)
    for g in range(table.shape[0] // pairs):
        mine = chosen == g
        for t in range(pairs // 8):
            at = g * pairs + t * 8
            totals[t] = jnp.where(mine, sums[at : at + 8], totals[t])
    return totals


def crossed_blocks(group, pairs, shift, orbits, masks, packed_ref, coded_ref, crossed_ref):
    me = lax.axis_index("cd")
    base = me * orbits
    lines = coded_ref.shape[1]
    step = min(lines, 4)

    def block(out, mask):
        slab = me ^ mask
        coded = coded_ref[slab]
        first = coded >> shift
        second = (coded & ((1 << shift) - 1)) - base
        here = jnp.logical_and(second >= 0, second < orbits)
        second = jnp.where(here, second, 0)
        groups = lax.div(second, jnp.int32(group))
        keys = (second - groups * group) * orbits + first
        groups = jnp.where(here, groups, -1)
        for i in range(0, lines, step):
            zero = [jnp.zeros((8, step * LANES), jnp.float32)] * (pairs // 8)
            got = lookup(packed_ref[slab], pairs, keys[i : i + step], groups[i : i + step], zero)
            crossed_ref[out, :, i * LANES : (i + step) * LANES] = jnp.concatenate(got, axis=0).astype(jnp.bfloat16)

    for at in range(0, len(masks), 2):
        some = list(range(at, min(at + 2, len(masks))))
        needed = functools.reduce(jnp.logical_or, [(me ^ masks[out]) <= me for out in some])

        @pl.when(needed)
        def _(some=some):
            for out in some:
                block(out, masks[out])

        @pl.when(jnp.logical_not(needed))
        def _(some=some):
            for out in some:
                crossed_ref[out] = jnp.zeros(crossed_ref.shape[1:], jnp.bfloat16)


def direct_kernel(group, pairs, shift, orbits, slabs, lower, upper, packed_ref, coded_ref, *refs):
    old_ref, direct_ref = refs[0], refs[-1]
    me = lax.axis_index("cd")
    upper_half = lax.div(me, jnp.int32(slabs // 2))
    begin = me + lower[0] + upper_half * (upper[0] - lower[0])
    end = lax.min(me + lower[1] + upper_half * (upper[1] - lower[1]), jnp.int32(slabs))
    direct_ref[...] = jnp.zeros(direct_ref.shape, jnp.bfloat16) if old_ref is None else old_ref[...]

    @pl.when(begin < end)
    def _():
        coded = coded_ref[...]
        first = coded >> shift
        second = coded & ((1 << shift) - 1)
        groups = lax.div(first, jnp.int32(group))
        owner = lax.div(second, jnp.int32(orbits))
        keys = (first - groups * group) * orbits + (second - owner * orbits)
        lines = coded.shape[0]
        step = min(lines, 4)

        def one(slab, carry):
            for i in range(0, lines, step):
                here = slice(i * LANES, (i + step) * LANES)
                old = direct_ref[:, here].astype(jnp.float32)
                got = [old[t * 8 : (t + 1) * 8] for t in range(pairs // 8)]
                chosen = jnp.where(owner[i : i + step] == slab, groups[i : i + step], -1)
                got = lookup(packed_ref[slab], pairs, keys[i : i + step], chosen, got)
                direct_ref[:, here] = jnp.concatenate(got, axis=0).astype(jnp.bfloat16)
            return carry

        lax.fori_loop(begin, end, one, 0)


def direct_first(*args):
    *head, direct_ref = args
    direct_kernel(*head, None, direct_ref)


def crossed_kernel(group, pairs, shift, orbits, masks, packed_ref, coded_ref, *refs):
    crossed_ref = refs[-1]
    crossed_blocks(group, pairs, shift, orbits, masks, packed_ref, coded_ref, crossed_ref)


def ladder_kernel(masks, parts, *refs):
    packed_refs, values_ref, out_ref = refs[:parts], refs[parts], refs[-1]
    width = out_ref.shape[2]
    me = lax.axis_index("cd")
    packed = jnp.concatenate([ref[...] for ref in packed_refs], axis=0)
    for out, mask in enumerate(masks):
        at = pl.ds(pl.multiple_of((me ^ mask) * width, width), width)
        out_ref[out] = lax.dot_general(
            values_ref[at, :],
            packed,
            (((1,), (1,)), ((), ())),
            preferred_element_type=jnp.float32,
        ).T.astype(out_ref.dtype)


def add_kernel(*refs):
    total = refs[0][...]
    for ref in refs[1:-1]:
        total = total + ref[...].astype(jnp.float32)
    refs[-1][...] = total


def add_up(total, parts):
    for part in parts[:-1]:
        total = pl.pallas_call(
            add_kernel,
            out_shape=jax.ShapeDtypeStruct(total.shape, total.dtype),
            in_specs=[VMEM] * 2,
            out_specs=VMEM,
            compiler_params=params(8),
            cost_estimate=spent(0.5),
            name="add",
        )(total, part)
    return total + parts[-1].astype(jnp.float32)


def on_device(pair_values, amplitudes, cd_first, cd_second, live_cols):
    slabs = lax.axis_size("cd")
    blocks = lax.axis_size("ab")
    pair_block, orbits, orbitals = amplitudes.shape
    columns = cd_first.shape[0]
    rows = pair_values.shape[0]
    lines = columns // LANES
    pairs = -(-pair_block // 16) * 16
    group = group_size(orbits)
    shift = (orbitals - 1).bit_length()
    near = list(range(0, slabs, 2))
    far = list(range(1, slabs, 2))

    coded, own_coded = pl.pallas_call(
        functools.partial(code_kernel, slabs, orbits, shift),
        out_shape=(
            jax.ShapeDtypeStruct((slabs, lines, LANES), jnp.int32),
            jax.ShapeDtypeStruct((lines, LANES), jnp.int32),
        ),
        in_specs=[HBM] * 2,
        out_specs=(VMEM, VMEM),
        scratch_shapes=[pltpu.VMEM((lines, LANES), jnp.int32)] * 2 + [pltpu.SemaphoreType.DMA((2,))],
        compiler_params=params(4),
        cost_estimate=spent(20),
        name="code",
    )(in_hbm(cd_first.reshape(lines, LANES)), in_hbm(cd_second.reshape(lines, LANES)))
    coded = lax.all_to_all(coded, "cd", split_axis=0, concat_axis=0, tiled=True)

    table = jnp.transpose(amplitudes, (1, 0, 2))
    if pairs != pair_block:
        table = jnp.pad(table, ((0, 0), (0, pairs - pair_block), (0, 0)))
    table = table.reshape(orbits * pairs, orbitals)
    packed_rows = orbits // group * pairs
    steps = 4 if orbits // group % 4 == 0 else 1
    table = pl.pallas_call(
        functools.partial(pack_kernel, slabs, orbits, group, pairs),
        out_shape=jax.ShapeDtypeStruct((slabs, packed_rows, DEPTH), jnp.bfloat16),
        in_specs=[HBM],
        out_specs=VMEM,
        scratch_shapes=[
            pltpu.VMEM((orbits * pairs, orbitals), jnp.bfloat16),
            pltpu.SemaphoreType.DMA((steps,)),
        ],
        compiler_params=params(16),
        cost_estimate=cost(0, 4 * orbits * pairs * orbitals),
        name="pack",
    )(in_hbm(table))

    lookup_flops = 2 * packed_rows * DEPTH * columns
    lookup_bytes = packed_rows * DEPTH * 2 + columns * pairs * 2

    def direct_for(lower, upper, *old):
        return pl.pallas_call(
            functools.partial(direct_kernel if old else direct_first, group, pairs, shift, orbits, slabs, lower, upper),
            out_shape=jax.ShapeDtypeStruct((pairs, columns), jnp.bfloat16),
            in_specs=[VMEM] * 2 + [VMEM, ANY][: len(old)],
            out_specs=VMEM,
            compiler_params=params(20),
            cost_estimate=SMALL if old else spent(2),
            name="direct",
        )(table, own_coded, *old)

    half = max(slabs // 2, 1)
    ends = [0, half - half // 4, 2 * (half - half // 4), slabs]
    direct = direct_for((ends[0], ends[1]), (0, 0))
    coded, direct = lax.optimization_barrier((coded, direct))

    def crossed_for(masks, name, *after):
        return pl.pallas_call(
            functools.partial(crossed_kernel, group, pairs, shift, orbits, masks),
            out_shape=jax.ShapeDtypeStruct((len(masks), pairs, columns), jnp.bfloat16),
            in_specs=[VMEM] * 2 + [ANY] * len(after),
            out_specs=VMEM,
            compiler_params=params(20),
            cost_estimate=SMALL,
            name=name,
        )(table, coded, *after)

    pairs_of = [near[at : at + 2] for at in reversed(range(0, slabs // 2, 2))]
    arrived, last = [], ()
    for masks in pairs_of:
        if arrived:
            direct = direct_for((ends[1], ends[2]), (0, 0), direct, *last)
            last = (direct,)
        last = (crossed_for([mask + 1 for mask in masks], "crossed_far", *last),)
        arrived.append(swap(last[0], "cd", slabs, 1))
    got = []
    for masks, block in zip(pairs_of, arrived):
        merged = crossed_for(masks, "crossed_near", *last) + block
        last = (merged,)
        for k in reversed(range(len(masks))):
            if masks[k]:
                got.append(swap(merged[k], "cd", slabs, masks[k]))
    direct = direct_for((ends[2], ends[3]), (0, slabs - half), direct, *last)
    crossed = add_up(merged[0].astype(jnp.float32), got)
    live_cols, _ = lax.optimization_barrier((live_cols, merged))
    slots = jnp.arange(columns, dtype=jnp.int32)
    live = (slots < live_cols[0]).astype(jnp.float32)
    weight = jnp.where(cd_first == cd_second, jnp.float32(0.5), jnp.float32(1.0)) * live
    packed = ((direct.astype(jnp.float32) + crossed) * weight[None, :]).astype(jnp.bfloat16)

    gathered = [lax.all_gather(packed[:pair_block], "ab", axis=0, tiled=True)]
    all_pairs = blocks * pair_block

    width = rows // slabs

    def ladder_for(masks, dtype, name, *after):
        return pl.pallas_call(
            functools.partial(ladder_kernel, masks, len(gathered)),
            out_shape=jax.ShapeDtypeStruct((len(masks), all_pairs, width), dtype),
            in_specs=[VMEM] * (len(gathered) + 1) + [ANY] * len(after),
            out_specs=VMEM,
            compiler_params=params(16),
            cost_estimate=SMALL,
            name=name,
        )(*gathered, pair_values, *after)

    got, last = [], ()
    for mask in reversed(near[1:]):
        last = (ladder_for([mask, mask + 1], jnp.bfloat16, "ladder", *last),)
        got.append(swap(last[0], "cd", slabs, mask))
    total = ladder_for([0, 1], jnp.float32, "ladder_own", *last)
    total = add_up(total, got)
    total = total[0] + swap(total[1].astype(jnp.bfloat16), "cd", slabs, 1).astype(jnp.float32)
    return total.astype(jnp.bfloat16)


def solution(mesh):
    placed = (P("ab", "cd"), P("ab", "cd", None), P("cd"), P("cd"), P("cd"))
    return jax.shard_map(
        on_device, mesh=mesh, in_specs=placed, out_specs=P(None, ("ab", "cd")), check_vma=False
    )
```

```python
import functools

import jax
import jax.numpy as jnp
from jax import lax
from jax.experimental import pallas as pl
from jax.experimental.pallas import tpu as pltpu
from jax.sharding import PartitionSpec as P

LANES = 128
DEPTH = 512
MIB = 1024 * 1024
VMEM = pl.BlockSpec(memory_space=pltpu.VMEM)
ANY = pl.BlockSpec(memory_space=pl.ANY)
HBM = pl.BlockSpec(memory_space=pltpu.HBM)


def group_size(orbits):
    return max(g for g in range(1, orbits + 1) if orbits % g == 0 and g * orbits <= DEPTH)


def params(mib):
    return pltpu.CompilerParams(vmem_limit_bytes=mib * MIB)


def cost(flops, bytes_accessed):
    return pl.CostEstimate(flops=flops, bytes_accessed=bytes_accessed, transcendentals=0)


def spent(microseconds):
    return cost(int(microseconds * 1.1e9), 1)


SMALL = spent(0.01)


def in_hbm(x):
    return pltpu.with_memory_space_constraint(x, pltpu.HBM)


def swap(x, axis, size, mask):
    return lax.ppermute(x, axis, [(i, i ^ mask) for i in range(size)])


def code_kernel(slabs, orbits, shift, first_ref, second_ref, coded_ref, own_ref, first_here, second_here, sems):
    copies = [
        pltpu.make_async_copy(first_ref, first_here, sems.at[0]),
        pltpu.make_async_copy(second_ref, second_here, sems.at[1]),
    ]
    for copy in copies:
        copy.start()
    for copy in copies:
        copy.wait()
    base = lax.axis_index("cd") * orbits
    coded = ((first_here[...] - base) << shift) + second_here[...]
    own_ref[...] = coded
    for s in range(slabs):
        coded_ref[s] = coded


def pack_kernel(slabs, orbits, group, pairs, table_ref, packed_ref, here_ref, sems):
    steps = sems.shape[0]
    rows = table_ref.shape[0] // steps
    copies = []
    for i in range(steps):
        at = pl.ds(i * rows, rows)
        copies.append(pltpu.make_async_copy(table_ref.at[at], here_ref.at[at], sems.at[i]))
        copies[i].start()
    per_step = rows // (group * pairs)
    for i in range(steps):
        copies[i].wait()
        for s in range(slabs):
            for g in range(i * per_step, (i + 1) * per_step):
                parts = [
                    here_ref[(g * group + k) * pairs : (g * group + k + 1) * pairs, s * orbits : (s + 1) * orbits]
                    for k in range(group)
                ]
                if group * orbits < DEPTH:
                    parts.append(jnp.zeros((pairs, DEPTH - group * orbits), jnp.bfloat16))
                packed_ref[s, g * pairs : (g + 1) * pairs, :] = jnp.concatenate(parts, axis=1)


def lookup(table, pairs, keys, groups, totals):
    per_row = keys.shape[0]
    width = per_row * LANES
    key = jnp.concatenate([keys[j : j + 1] for j in range(per_row)], axis=1)
    chosen = jnp.concatenate([groups[j : j + 1] for j in range(per_row)], axis=1)
    hot = jnp.where(lax.broadcasted_iota(jnp.int32, (DEPTH, width), 0) == key, 1.0, 0.0).astype(jnp.bfloat16)
    sums = jnp.dot(table, hot, preferred_element_type=jnp.float32)
    chosen = jnp.broadcast_to(chosen, (8, width))
    totals = list(totals)
    for g in range(table.shape[0] // pairs):
        mine = chosen == g
        for t in range(pairs // 8):
            at = g * pairs + t * 8
            totals[t] = jnp.where(mine, sums[at : at + 8], totals[t])
    return totals


def crossed_blocks(group, pairs, shift, orbits, masks, packed_ref, coded_ref, crossed_ref):
    me = lax.axis_index("cd")
    base = me * orbits
    lines = coded_ref.shape[1]
    step = min(lines, 4)

    def block(out, mask):
        slab = me ^ mask
        coded = coded_ref[slab]
        first = coded >> shift
        second = (coded & ((1 << shift) - 1)) - base
        here = jnp.logical_and(second >= 0, second < orbits)
        second = jnp.where(here, second, 0)
        groups = lax.div(second, jnp.int32(group))
        keys = (second - groups * group) * orbits + first
        groups = jnp.where(here, groups, -1)
        for i in range(0, lines, step):
            zero = [jnp.zeros((8, step * LANES), jnp.float32)] * (pairs // 8)
            got = lookup(packed_ref[slab], pairs, keys[i : i + step], groups[i : i + step], zero)
            crossed_ref[out, :, i * LANES : (i + step) * LANES] = jnp.concatenate(got, axis=0).astype(jnp.bfloat16)

    for at in range(0, len(masks), 2):
        some = list(range(at, min(at + 2, len(masks))))
        needed = functools.reduce(jnp.logical_or, [(me ^ masks[out]) <= me for out in some])

        @pl.when(needed)
        def _(some=some):
            for out in some:
                block(out, masks[out])

        @pl.when(jnp.logical_not(needed))
        def _(some=some):
            for out in some:
                crossed_ref[out] = jnp.zeros(crossed_ref.shape[1:], jnp.bfloat16)


def direct_kernel(group, pairs, shift, orbits, slabs, shares, packed_ref, coded_ref, *refs):
    old_ref, direct_ref = refs[0], refs[-1]
    me = lax.axis_index("cd")
    begin = end = jnp.int32(0)
    for k, (low, high) in enumerate(shares):
        begin = jnp.where(me == k, jnp.int32(low), begin)
        end = jnp.where(me == k, jnp.int32(high), end)
    direct_ref[...] = jnp.zeros(direct_ref.shape, jnp.bfloat16) if old_ref is None else old_ref[...]

    @pl.when(begin < end)
    def _():
        coded = coded_ref[...]
        first = coded >> shift
        second = coded & ((1 << shift) - 1)
        groups = lax.div(first, jnp.int32(group))
        owner = lax.div(second, jnp.int32(orbits))
        keys = (first - groups * group) * orbits + (second - owner * orbits)
        lines = coded.shape[0]
        step = min(lines, 4)

        def one(slab, carry):
            for i in range(0, lines, step):
                here = slice(i * LANES, (i + step) * LANES)
                old = direct_ref[:, here].astype(jnp.float32)
                got = [old[t * 8 : (t + 1) * 8] for t in range(pairs // 8)]
                chosen = jnp.where(owner[i : i + step] == slab, groups[i : i + step], -1)
                got = lookup(packed_ref[slab], pairs, keys[i : i + step], chosen, got)
                direct_ref[:, here] = jnp.concatenate(got, axis=0).astype(jnp.bfloat16)
            return carry

        lax.fori_loop(begin, end, one, 0)


def direct_first(*args):
    *head, direct_ref = args
    direct_kernel(*head, None, direct_ref)


def crossed_kernel(group, pairs, shift, orbits, masks, packed_ref, coded_ref, *refs):
    crossed_ref = refs[-1]
    crossed_blocks(group, pairs, shift, orbits, masks, packed_ref, coded_ref, crossed_ref)


def ladder_kernel(masks, parts, *refs):
    packed_refs, values_ref, out_ref = refs[:parts], refs[parts], refs[-1]
    width = out_ref.shape[2]
    me = lax.axis_index("cd")
    packed = jnp.concatenate([ref[...] for ref in packed_refs], axis=0)
    for out, mask in enumerate(masks):
        at = pl.ds(pl.multiple_of((me ^ mask) * width, width), width)
        out_ref[out] = lax.dot_general(
            values_ref[at, :],
            packed,
            (((1,), (1,)), ((), ())),
            preferred_element_type=jnp.float32,
        ).T.astype(out_ref.dtype)


def add_kernel(*refs):
    total = refs[0][...]
    for ref in refs[1:-1]:
        total = total + ref[...].astype(jnp.float32)
    refs[-1][...] = total


def add_up(total, parts, weight):
    for part in parts[:-1]:
        total = pl.pallas_call(
            add_kernel,
            out_shape=jax.ShapeDtypeStruct(total.shape, total.dtype),
            in_specs=[VMEM] * 2,
            out_specs=VMEM,
            compiler_params=params(8),
            cost_estimate=spent(weight),
            name="add",
        )(total, part)
    return total + parts[-1].astype(jnp.float32)


def on_device(pair_values, amplitudes, cd_first, cd_second, live_cols):
    slabs = lax.axis_size("cd")
    blocks = lax.axis_size("ab")
    pair_block, orbits, orbitals = amplitudes.shape
    columns = cd_first.shape[0]
    rows = pair_values.shape[0]
    lines = columns // LANES
    pairs = -(-pair_block // 16) * 16
    group = group_size(orbits)
    shift = (orbitals - 1).bit_length()
    near = list(range(0, slabs, 2))
    far = list(range(1, slabs, 2))

    coded, own_coded = pl.pallas_call(
        functools.partial(code_kernel, slabs, orbits, shift),
        out_shape=(
            jax.ShapeDtypeStruct((slabs, lines, LANES), jnp.int32),
            jax.ShapeDtypeStruct((lines, LANES), jnp.int32),
        ),
        in_specs=[HBM] * 2,
        out_specs=(VMEM, VMEM),
        scratch_shapes=[pltpu.VMEM((lines, LANES), jnp.int32)] * 2 + [pltpu.SemaphoreType.DMA((2,))],
        compiler_params=params(4),
        cost_estimate=spent(20),
        name="code",
    )(in_hbm(cd_first.reshape(lines, LANES)), in_hbm(cd_second.reshape(lines, LANES)))
    coded = lax.all_to_all(coded, "cd", split_axis=0, concat_axis=0, tiled=True)

    table = jnp.transpose(amplitudes, (1, 0, 2))
    if pairs != pair_block:
        table = jnp.pad(table, ((0, 0), (0, pairs - pair_block), (0, 0)))
    table = table.reshape(orbits * pairs, orbitals)
    packed_rows = orbits // group * pairs
    steps = 4 if orbits // group % 4 == 0 else 1
    table = pl.pallas_call(
        functools.partial(pack_kernel, slabs, orbits, group, pairs),
        out_shape=jax.ShapeDtypeStruct((slabs, packed_rows, DEPTH), jnp.bfloat16),
        in_specs=[HBM],
        out_specs=VMEM,
        scratch_shapes=[
            pltpu.VMEM((orbits * pairs, orbitals), jnp.bfloat16),
            pltpu.SemaphoreType.DMA((steps,)),
        ],
        compiler_params=params(16),
        cost_estimate=cost(0, 4 * orbits * pairs * orbitals),
        name="pack",
    )(in_hbm(table))

    lookup_flops = 2 * packed_rows * DEPTH * columns
    lookup_bytes = packed_rows * DEPTH * 2 + columns * pairs * 2

    def direct_for(part, *old):
        return pl.pallas_call(
            functools.partial(direct_kernel if old else direct_first, group, pairs, shift, orbits, slabs, shares[part]),
            out_shape=jax.ShapeDtypeStruct((pairs, columns), jnp.bfloat16),
            in_specs=[VMEM] * 2 + [VMEM, ANY][: len(old)],
            out_specs=VMEM,
            compiler_params=params(20),
            cost_estimate=SMALL if old else spent(2),
            name="direct",
        )(table, own_coded, *old)

    half = slabs // 2
    first = [half - half // 4 if k < half else 0 for k in range(slabs)]
    second = [first[0] if k == 0 else half // 2 if k == half else 0 for k in range(slabs)]
    shares = [
        [(k, k + first[k]) for k in range(slabs)],
        [(k + first[k], k + first[k] + second[k]) for k in range(slabs)],
        [(k + first[k] + second[k], slabs) for k in range(slabs)],
    ]
    direct = direct_for(0)
    coded, direct = lax.optimization_barrier((coded, direct))

    def crossed_for(masks, name, *after):
        return pl.pallas_call(
            functools.partial(crossed_kernel, group, pairs, shift, orbits, masks),
            out_shape=jax.ShapeDtypeStruct((len(masks), pairs, columns), jnp.bfloat16),
            in_specs=[VMEM] * 2 + [ANY] * len(after),
            out_specs=VMEM,
            compiler_params=params(20),
            cost_estimate=SMALL,
            name=name,
        )(table, coded, *after)

    pairs_of = [near[at : at + 2] for at in reversed(range(0, slabs // 2, 2))]
    arrived, last = [], ()
    for masks in pairs_of:
        if arrived:
            direct = direct_for(1, direct, *last)
            last = (direct,)
        last = (crossed_for([mask + 1 for mask in masks], "crossed_far", *last),)
        arrived.append(swap(last[0], "cd", slabs, 1))
    got = []
    for masks, block in zip(pairs_of, arrived):
        merged = crossed_for(masks, "crossed_near", *last) + block
        last = (merged,)
        for k in reversed(range(len(masks))):
            if masks[k]:
                got.append(swap(merged[k], "cd", slabs, masks[k]))
    direct = direct_for(2, direct, *last)
    crossed = add_up(merged[0].astype(jnp.float32), got, 0.5)
    live_cols, _ = lax.optimization_barrier((live_cols, merged))
    slots = jnp.arange(columns, dtype=jnp.int32)
    live = (slots < live_cols[0]).astype(jnp.float32)
    weight = jnp.where(cd_first == cd_second, jnp.float32(0.5), jnp.float32(1.0)) * live
    packed = ((direct.astype(jnp.float32) + crossed) * weight[None, :]).astype(jnp.bfloat16)

    gathered = [lax.all_gather(packed[:pair_block], "ab", axis=0, tiled=True)]
    all_pairs = blocks * pair_block

    width = rows // slabs

    def ladder_for(masks, dtype, name, *after):
        return pl.pallas_call(
            functools.partial(ladder_kernel, masks, len(gathered)),
            out_shape=jax.ShapeDtypeStruct((len(masks), all_pairs, width), dtype),
            in_specs=[VMEM] * (len(gathered) + 1) + [ANY] * len(after),
            out_specs=VMEM,
            compiler_params=params(16),
            cost_estimate=SMALL,
            name=name,
        )(*gathered, pair_values, *after)

    arrived, last = [], ()
    for masks in pairs_of:
        last = (ladder_for([mask + 1 for mask in masks], jnp.bfloat16, "ladder_far", *last),)
        arrived.append(swap(last[0], "cd", slabs, 1))
    got = []
    for masks, block in zip(pairs_of, arrived):
        merged = ladder_for(masks, jnp.float32, "ladder_near", *last) + block.astype(jnp.float32)
        sent = merged.astype(jnp.bfloat16)
        last = (sent,)
        for k in reversed(range(len(masks))):
            if masks[k]:
                got.append(swap(sent[k], "cd", slabs, masks[k]))
    return add_up(merged[0], got, 0.02).astype(jnp.bfloat16)


def solution(mesh):
    placed = (P("ab", "cd"), P("ab", "cd", None), P("cd"), P("cd"), P("cd"))
    return jax.shard_map(
        on_device, mesh=mesh, in_specs=placed, out_specs=P(None, ("ab", "cd")), check_vma=False
    )
```

```python
import functools

import jax
import jax.numpy as jnp
from jax import lax
from jax.experimental import pallas as pl
from jax.experimental.pallas import tpu as pltpu
from jax.sharding import PartitionSpec as P

LANES = 128
DEPTH = 512
MIB = 1024 * 1024
VMEM = pl.BlockSpec(memory_space=pltpu.VMEM)
ANY = pl.BlockSpec(memory_space=pl.ANY)
HBM = pl.BlockSpec(memory_space=pltpu.HBM)


def group_size(orbits):
    return max(g for g in range(1, orbits + 1) if orbits % g == 0 and g * orbits <= DEPTH)


def params(mib):
    return pltpu.CompilerParams(vmem_limit_bytes=mib * MIB)


def cost(flops, bytes_accessed):
    return pl.CostEstimate(flops=flops, bytes_accessed=bytes_accessed, transcendentals=0)


def spent(microseconds):
    return cost(int(microseconds * 1.1e9), 1)


SMALL = spent(0.01)


def in_hbm(x):
    return pltpu.with_memory_space_constraint(x, pltpu.HBM)


def swap(x, axis, size, mask):
    return lax.ppermute(x, axis, [(i, i ^ mask) for i in range(size)])


def code_kernel(slabs, orbits, shift, first_ref, second_ref, coded_ref, own_ref, first_here, second_here, sems):
    copies = [
        pltpu.make_async_copy(first_ref, first_here, sems.at[0]),
        pltpu.make_async_copy(second_ref, second_here, sems.at[1]),
    ]
    for copy in copies:
        copy.start()
    for copy in copies:
        copy.wait()
    base = lax.axis_index("cd") * orbits
    coded = ((first_here[...] - base) << shift) + second_here[...]
    own_ref[...] = coded
    for s in range(slabs):
        coded_ref[s] = coded


def pack_kernel(slabs, orbits, group, pairs, table_ref, packed_ref, here_ref, sems):
    steps = sems.shape[0]
    rows = table_ref.shape[0] // steps
    copies = []
    for i in range(steps):
        at = pl.ds(i * rows, rows)
        copies.append(pltpu.make_async_copy(table_ref.at[at], here_ref.at[at], sems.at[i]))
        copies[i].start()
    per_step = rows // (group * pairs)
    for i in range(steps):
        copies[i].wait()
        for s in range(slabs):
            for g in range(i * per_step, (i + 1) * per_step):
                parts = [
                    here_ref[(g * group + k) * pairs : (g * group + k + 1) * pairs, s * orbits : (s + 1) * orbits]
                    for k in range(group)
                ]
                if group * orbits < DEPTH:
                    parts.append(jnp.zeros((pairs, DEPTH - group * orbits), jnp.bfloat16))
                packed_ref[s, g * pairs : (g + 1) * pairs, :] = jnp.concatenate(parts, axis=1)


def lookup(table, pairs, keys, groups, totals):
    per_row = keys.shape[0]
    width = per_row * LANES
    key = jnp.concatenate([keys[j : j + 1] for j in range(per_row)], axis=1)
    chosen = jnp.concatenate([groups[j : j + 1] for j in range(per_row)], axis=1)
    hot = jnp.where(lax.broadcasted_iota(jnp.int32, (DEPTH, width), 0) == key, 1.0, 0.0).astype(jnp.bfloat16)
    sums = jnp.dot(table, hot, preferred_element_type=jnp.float32)
    chosen = jnp.broadcast_to(chosen, (8, width))
    totals = list(totals)
    for g in range(table.shape[0] // pairs):
        mine = chosen == g
        for t in range(pairs // 8):
            at = g * pairs + t * 8
            totals[t] = jnp.where(mine, sums[at : at + 8], totals[t])
    return totals


def crossed_blocks(group, pairs, shift, orbits, masks, packed_ref, coded_ref, crossed_ref):
    me = lax.axis_index("cd")
    base = me * orbits
    lines = coded_ref.shape[1]
    step = min(lines, 4)

    def block(out, mask):
        slab = me ^ mask
        coded = coded_ref[slab]
        first = coded >> shift
        second = (coded & ((1 << shift) - 1)) - base
        here = jnp.logical_and(second >= 0, second < orbits)
        second = jnp.where(here, second, 0)
        groups = lax.div(second, jnp.int32(group))
        keys = (second - groups * group) * orbits + first
        groups = jnp.where(here, groups, -1)
        for i in range(0, lines, step):
            zero = [jnp.zeros((8, step * LANES), jnp.float32)] * (pairs // 8)
            got = lookup(packed_ref[slab], pairs, keys[i : i + step], groups[i : i + step], zero)
            crossed_ref[out, :, i * LANES : (i + step) * LANES] = jnp.concatenate(got, axis=0).astype(jnp.bfloat16)

    for at in range(0, len(masks), 2):
        some = list(range(at, min(at + 2, len(masks))))
        needed = functools.reduce(jnp.logical_or, [(me ^ masks[out]) <= me for out in some])

        @pl.when(needed)
        def _(some=some):
            for out in some:
                block(out, masks[out])

        @pl.when(jnp.logical_not(needed))
        def _(some=some):
            for out in some:
                crossed_ref[out] = jnp.zeros(crossed_ref.shape[1:], jnp.bfloat16)


def direct_kernel(group, pairs, shift, orbits, slabs, shares, packed_ref, coded_ref, *refs):
    old_ref, direct_ref = refs[0], refs[-1]
    me = lax.axis_index("cd")
    begin = end = jnp.int32(0)
    for k, (low, high) in enumerate(shares):
        begin = jnp.where(me == k, jnp.int32(low), begin)
        end = jnp.where(me == k, jnp.int32(high), end)
    direct_ref[...] = jnp.zeros(direct_ref.shape, jnp.bfloat16) if old_ref is None else old_ref[...]

    @pl.when(begin < end)
    def _():
        coded = coded_ref[...]
        first = coded >> shift
        second = coded & ((1 << shift) - 1)
        groups = lax.div(first, jnp.int32(group))
        owner = lax.div(second, jnp.int32(orbits))
        keys = (first - groups * group) * orbits + (second - owner * orbits)
        lines = coded.shape[0]
        step = min(lines, 4)

        def one(slab, carry):
            for i in range(0, lines, step):
                here = slice(i * LANES, (i + step) * LANES)
                old = direct_ref[:, here].astype(jnp.float32)
                got = [old[t * 8 : (t + 1) * 8] for t in range(pairs // 8)]
                chosen = jnp.where(owner[i : i + step] == slab, groups[i : i + step], -1)
                got = lookup(packed_ref[slab], pairs, keys[i : i + step], chosen, got)
                direct_ref[:, here] = jnp.concatenate(got, axis=0).astype(jnp.bfloat16)
            return carry

        lax.fori_loop(begin, end, one, 0)


def direct_first(*args):
    *head, direct_ref = args
    direct_kernel(*head, None, direct_ref)


def crossed_kernel(group, pairs, shift, orbits, masks, packed_ref, coded_ref, *refs):
    crossed_ref = refs[-1]
    crossed_blocks(group, pairs, shift, orbits, masks, packed_ref, coded_ref, crossed_ref)


def ladder_kernel(masks, parts, *refs):
    packed_refs, values_ref, out_ref = refs[:parts], refs[parts], refs[-1]
    width = out_ref.shape[2]
    me = lax.axis_index("cd")
    packed = jnp.concatenate([ref[...] for ref in packed_refs], axis=0)
    for out, mask in enumerate(masks):
        at = pl.ds(pl.multiple_of((me ^ mask) * width, width), width)
        out_ref[out] = lax.dot_general(
            values_ref[at, :],
            packed,
            (((1,), (1,)), ((), ())),
            preferred_element_type=jnp.float32,
        ).T.astype(out_ref.dtype)


def add_kernel(*refs):
    total = refs[0][...]
    for ref in refs[1:-1]:
        total = total + ref[...].astype(jnp.float32)
    refs[-1][...] = total


def add_up(total, parts, weight):
    for part in parts[:-1]:
        total = pl.pallas_call(
            add_kernel,
            out_shape=jax.ShapeDtypeStruct(total.shape, total.dtype),
            in_specs=[VMEM] * 2,
            out_specs=VMEM,
            compiler_params=params(8),
            cost_estimate=spent(weight),
            name="add",
        )(total, part)
    return total + parts[-1].astype(jnp.float32)


def on_device(pair_values, amplitudes, cd_first, cd_second, live_cols):
    slabs = lax.axis_size("cd")
    blocks = lax.axis_size("ab")
    pair_block, orbits, orbitals = amplitudes.shape
    columns = cd_first.shape[0]
    rows = pair_values.shape[0]
    lines = columns // LANES
    pairs = -(-pair_block // 16) * 16
    group = group_size(orbits)
    shift = (orbitals - 1).bit_length()
    near = list(range(0, slabs, 2))
    far = list(range(1, slabs, 2))

    coded, own_coded = pl.pallas_call(
        functools.partial(code_kernel, slabs, orbits, shift),
        out_shape=(
            jax.ShapeDtypeStruct((slabs, lines, LANES), jnp.int32),
            jax.ShapeDtypeStruct((lines, LANES), jnp.int32),
        ),
        in_specs=[HBM] * 2,
        out_specs=(VMEM, VMEM),
        scratch_shapes=[pltpu.VMEM((lines, LANES), jnp.int32)] * 2 + [pltpu.SemaphoreType.DMA((2,))],
        compiler_params=params(4),
        cost_estimate=spent(20),
        name="code",
    )(in_hbm(cd_first.reshape(lines, LANES)), in_hbm(cd_second.reshape(lines, LANES)))
    coded = lax.all_to_all(coded, "cd", split_axis=0, concat_axis=0, tiled=True)

    table = jnp.transpose(amplitudes, (1, 0, 2))
    if pairs != pair_block:
        table = jnp.pad(table, ((0, 0), (0, pairs - pair_block), (0, 0)))
    table = table.reshape(orbits * pairs, orbitals)
    packed_rows = orbits // group * pairs
    steps = 4 if orbits // group % 4 == 0 else 1
    table = pl.pallas_call(
        functools.partial(pack_kernel, slabs, orbits, group, pairs),
        out_shape=jax.ShapeDtypeStruct((slabs, packed_rows, DEPTH), jnp.bfloat16),
        in_specs=[HBM],
        out_specs=VMEM,
        scratch_shapes=[
            pltpu.VMEM((orbits * pairs, orbitals), jnp.bfloat16),
            pltpu.SemaphoreType.DMA((steps,)),
        ],
        compiler_params=params(16),
        cost_estimate=cost(0, 4 * orbits * pairs * orbitals),
        name="pack",
    )(in_hbm(table))

    lookup_flops = 2 * packed_rows * DEPTH * columns
    lookup_bytes = packed_rows * DEPTH * 2 + columns * pairs * 2

    def direct_for(part, *old):
        return pl.pallas_call(
            functools.partial(direct_kernel if old else direct_first, group, pairs, shift, orbits, slabs, shares[part]),
            out_shape=jax.ShapeDtypeStruct((pairs, columns), jnp.bfloat16),
            in_specs=[VMEM] * 2 + [VMEM, ANY][: len(old)],
            out_specs=VMEM,
            compiler_params=params(20),
            cost_estimate=SMALL if old else spent(2),
            name="direct",
        )(table, own_coded, *old)

    half = slabs // 2
    first = [half - half // 4 if k < half else 0 for k in range(slabs)]
    early = {0: first[0], 1: first[0] // 2, half: half // 2}
    second = [early.get(k, 0) for k in range(slabs)]
    shares = [
        [(k, k + first[k]) for k in range(slabs)],
        [(k + first[k], k + first[k] + second[k]) for k in range(slabs)],
        [(k + first[k] + second[k], slabs) for k in range(slabs)],
    ]
    direct = direct_for(0)
    coded, direct = lax.optimization_barrier((coded, direct))

    def crossed_for(masks, name, *after):
        return pl.pallas_call(
            functools.partial(crossed_kernel, group, pairs, shift, orbits, masks),
            out_shape=jax.ShapeDtypeStruct((len(masks), pairs, columns), jnp.bfloat16),
            in_specs=[VMEM] * 2 + [ANY] * len(after),
            out_specs=VMEM,
            compiler_params=params(20),
            cost_estimate=SMALL,
            name=name,
        )(table, coded, *after)

    pairs_of = [near[at : at + 2] for at in reversed(range(0, slabs // 2, 2))]
    arrived, last = [], ()
    for masks in pairs_of:
        if arrived:
            direct = direct_for(1, direct, *last)
            last = (direct,)
        last = (crossed_for([mask + 1 for mask in masks], "crossed_far", *last),)
        arrived.append(swap(last[0], "cd", slabs, 1))
    got = []
    for masks, block in zip(pairs_of, arrived):
        merged = crossed_for(masks, "crossed_near", *last) + block
        last = (merged,)
        for k in reversed(range(len(masks))):
            if masks[k]:
                got.append(swap(merged[k], "cd", slabs, masks[k]))
    direct = direct_for(2, direct, *last)
    crossed = add_up(merged[0].astype(jnp.float32), got, 0.5)
    live_cols, _ = lax.optimization_barrier((live_cols, merged))
    slots = jnp.arange(columns, dtype=jnp.int32)
    live = (slots < live_cols[0]).astype(jnp.float32)
    weight = jnp.where(cd_first == cd_second, jnp.float32(0.5), jnp.float32(1.0)) * live
    packed = ((direct.astype(jnp.float32) + crossed) * weight[None, :]).astype(jnp.bfloat16)

    gathered = [lax.all_gather(packed[:pair_block], "ab", axis=0, tiled=True)]
    all_pairs = blocks * pair_block

    width = rows // slabs

    def ladder_for(masks, dtype, name, *after):
        return pl.pallas_call(
            functools.partial(ladder_kernel, masks, len(gathered)),
            out_shape=jax.ShapeDtypeStruct((len(masks), all_pairs, width), dtype),
            in_specs=[VMEM] * (len(gathered) + 1) + [ANY] * len(after),
            out_specs=VMEM,
            compiler_params=params(16),
            cost_estimate=SMALL,
            name=name,
        )(*gathered, pair_values, *after)

    arrived, last = [], ()
    for masks in pairs_of:
        last = (ladder_for([mask + 1 for mask in masks], jnp.bfloat16, "ladder_far", *last),)
        arrived.append(swap(last[0], "cd", slabs, 1))
    got = []
    for masks, block in zip(pairs_of, arrived):
        own = ladder_for(masks, jnp.float32, "ladder_near", *last)
        last = (own,)
        merged = own + block.astype(jnp.float32)
        sent = merged.astype(jnp.bfloat16)
        for k in reversed(range(len(masks))):
            if masks[k]:
                got.append(swap(sent[k], "cd", slabs, masks[k]))
    return add_up(merged[0], got, 0.02).astype(jnp.bfloat16)


def solution(mesh):
    placed = (P("ab", "cd"), P("ab", "cd", None), P("cd"), P("cd"), P("cd"))
    return jax.shard_map(
        on_device, mesh=mesh, in_specs=placed, out_specs=P(None, ("ab", "cd")), check_vma=False
    )
```

```python
import functools

import jax
import jax.numpy as jnp
from jax import lax
from jax.experimental import pallas as pl
from jax.experimental.pallas import tpu as pltpu
from jax.sharding import PartitionSpec as P

LANES = 128
DEPTH = 512
MIB = 1024 * 1024
VMEM = pl.BlockSpec(memory_space=pltpu.VMEM)
ANY = pl.BlockSpec(memory_space=pl.ANY)
HBM = pl.BlockSpec(memory_space=pltpu.HBM)


def group_size(orbits):
    return max(g for g in range(1, orbits + 1) if orbits % g == 0 and g * orbits <= DEPTH)


def params(mib):
    return pltpu.CompilerParams(vmem_limit_bytes=mib * MIB)


def cost(flops, bytes_accessed):
    return pl.CostEstimate(flops=flops, bytes_accessed=bytes_accessed, transcendentals=0)


def spent(microseconds):
    return cost(int(microseconds * 1.1e9), 1)


SMALL = spent(0.01)


def in_hbm(x):
    return pltpu.with_memory_space_constraint(x, pltpu.HBM)


def swap(x, axis, size, mask):
    return lax.ppermute(x, axis, [(i, i ^ mask) for i in range(size)])


def code_kernel(slabs, orbits, shift, first_ref, second_ref, coded_ref, own_ref, first_here, second_here, sems):
    copies = [
        pltpu.make_async_copy(first_ref, first_here, sems.at[0]),
        pltpu.make_async_copy(second_ref, second_here, sems.at[1]),
    ]
    for copy in copies:
        copy.start()
    for copy in copies:
        copy.wait()
    base = lax.axis_index("cd") * orbits
    coded = ((first_here[...] - base) << shift) + second_here[...]
    own_ref[...] = coded
    for s in range(slabs):
        coded_ref[s] = coded


def pack_kernel(slabs, orbits, group, pairs, table_ref, packed_ref, here_ref, sems):
    steps = sems.shape[0]
    rows = table_ref.shape[0] // steps
    copies = []
    for i in range(steps):
        at = pl.ds(i * rows, rows)
        copies.append(pltpu.make_async_copy(table_ref.at[at], here_ref.at[at], sems.at[i]))
        copies[i].start()
    per_step = rows // (group * pairs)
    for i in range(steps):
        copies[i].wait()
        for s in range(slabs):
            for g in range(i * per_step, (i + 1) * per_step):
                parts = [
                    here_ref[(g * group + k) * pairs : (g * group + k + 1) * pairs, s * orbits : (s + 1) * orbits]
                    for k in range(group)
                ]
                if group * orbits < DEPTH:
                    parts.append(jnp.zeros((pairs, DEPTH - group * orbits), jnp.bfloat16))
                packed_ref[s, g * pairs : (g + 1) * pairs, :] = jnp.concatenate(parts, axis=1)


def lookup(table, pairs, keys, groups, totals):
    per_row = keys.shape[0]
    width = per_row * LANES
    key = jnp.concatenate([keys[j : j + 1] for j in range(per_row)], axis=1)
    chosen = jnp.concatenate([groups[j : j + 1] for j in range(per_row)], axis=1)
    hot = jnp.where(lax.broadcasted_iota(jnp.int32, (DEPTH, width), 0) == key, 1.0, 0.0).astype(jnp.bfloat16)
    sums = jnp.dot(table, hot, preferred_element_type=jnp.float32)
    chosen = jnp.broadcast_to(chosen, (8, width))
    totals = list(totals)
    for g in range(table.shape[0] // pairs):
        mine = chosen == g
        for t in range(pairs // 8):
            at = g * pairs + t * 8
            totals[t] = jnp.where(mine, sums[at : at + 8], totals[t])
    return totals


def crossed_blocks(group, pairs, shift, orbits, masks, packed_ref, coded_ref, crossed_ref):
    me = lax.axis_index("cd")
    base = me * orbits
    lines = coded_ref.shape[1]
    step = min(lines, 4)

    def block(out, mask):
        slab = me ^ mask
        coded = coded_ref[slab]
        first = coded >> shift
        second = (coded & ((1 << shift) - 1)) - base
        here = jnp.logical_and(second >= 0, second < orbits)
        second = jnp.where(here, second, 0)
        groups = lax.div(second, jnp.int32(group))
        keys = (second - groups * group) * orbits + first
        groups = jnp.where(here, groups, -1)
        for i in range(0, lines, step):
            zero = [jnp.zeros((8, step * LANES), jnp.float32)] * (pairs // 8)
            got = lookup(packed_ref[slab], pairs, keys[i : i + step], groups[i : i + step], zero)
            crossed_ref[out, :, i * LANES : (i + step) * LANES] = jnp.concatenate(got, axis=0).astype(jnp.bfloat16)

    for at in range(0, len(masks), 2):
        some = list(range(at, min(at + 2, len(masks))))
        needed = functools.reduce(jnp.logical_or, [(me ^ masks[out]) <= me for out in some])

        @pl.when(needed)
        def _(some=some):
            for out in some:
                block(out, masks[out])

        @pl.when(jnp.logical_not(needed))
        def _(some=some):
            for out in some:
                crossed_ref[out] = jnp.zeros(crossed_ref.shape[1:], jnp.bfloat16)


def direct_kernel(group, pairs, shift, orbits, slabs, shares, packed_ref, coded_ref, *refs):
    old_ref, direct_ref = refs[0], refs[-1]
    me = lax.axis_index("cd")
    begin = end = jnp.int32(0)
    for k, (low, high) in enumerate(shares):
        begin = jnp.where(me == k, jnp.int32(low), begin)
        end = jnp.where(me == k, jnp.int32(high), end)
    direct_ref[...] = jnp.zeros(direct_ref.shape, jnp.bfloat16) if old_ref is None else old_ref[...]

    @pl.when(begin < end)
    def _():
        coded = coded_ref[...]
        first = coded >> shift
        second = coded & ((1 << shift) - 1)
        groups = lax.div(first, jnp.int32(group))
        owner = lax.div(second, jnp.int32(orbits))
        keys = (first - groups * group) * orbits + (second - owner * orbits)
        lines = coded.shape[0]
        step = min(lines, 4)

        def one(slab, carry):
            for i in range(0, lines, step):
                here = slice(i * LANES, (i + step) * LANES)
                old = direct_ref[:, here].astype(jnp.float32)
                got = [old[t * 8 : (t + 1) * 8] for t in range(pairs // 8)]
                chosen = jnp.where(owner[i : i + step] == slab, groups[i : i + step], -1)
                got = lookup(packed_ref[slab], pairs, keys[i : i + step], chosen, got)
                direct_ref[:, here] = jnp.concatenate(got, axis=0).astype(jnp.bfloat16)
            return carry

        lax.fori_loop(begin, end, one, 0)


def direct_first(*args):
    *head, direct_ref = args
    direct_kernel(*head, None, direct_ref)


def crossed_kernel(group, pairs, shift, orbits, masks, packed_ref, coded_ref, *refs):
    crossed_ref = refs[-1]
    crossed_blocks(group, pairs, shift, orbits, masks, packed_ref, coded_ref, crossed_ref)


def ladder_kernel(masks, parts, *refs):
    packed_refs, values_ref, out_ref = refs[:parts], refs[parts], refs[-1]
    width = out_ref.shape[2]
    me = lax.axis_index("cd")
    packed = jnp.concatenate([ref[...] for ref in packed_refs], axis=0)
    for out, mask in enumerate(masks):
        at = pl.ds(pl.multiple_of((me ^ mask) * width, width), width)
        out_ref[out] = lax.dot_general(
            values_ref[at, :],
            packed,
            (((1,), (1,)), ((), ())),
            preferred_element_type=jnp.float32,
        ).T.astype(out_ref.dtype)


def add_kernel(*refs):
    total = refs[0][...]
    for ref in refs[1:-1]:
        total = total + ref[...].astype(jnp.float32)
    refs[-1][...] = total


def add_up(total, parts, weight):
    for part in parts[:-1]:
        total = pl.pallas_call(
            add_kernel,
            out_shape=jax.ShapeDtypeStruct(total.shape, total.dtype),
            in_specs=[VMEM] * 2,
            out_specs=VMEM,
            compiler_params=params(8),
            cost_estimate=spent(weight),
            name="add",
        )(total, part)
    return total + parts[-1].astype(jnp.float32)


def on_device(pair_values, amplitudes, cd_first, cd_second, live_cols):
    slabs = lax.axis_size("cd")
    blocks = lax.axis_size("ab")
    pair_block, orbits, orbitals = amplitudes.shape
    columns = cd_first.shape[0]
    rows = pair_values.shape[0]
    lines = columns // LANES
    pairs = -(-pair_block // 16) * 16
    group = group_size(orbits)
    shift = (orbitals - 1).bit_length()
    near = list(range(0, slabs, 2))
    far = list(range(1, slabs, 2))

    coded, own_coded = pl.pallas_call(
        functools.partial(code_kernel, slabs, orbits, shift),
        out_shape=(
            jax.ShapeDtypeStruct((slabs, lines, LANES), jnp.int32),
            jax.ShapeDtypeStruct((lines, LANES), jnp.int32),
        ),
        in_specs=[HBM] * 2,
        out_specs=(VMEM, VMEM),
        scratch_shapes=[pltpu.VMEM((lines, LANES), jnp.int32)] * 2 + [pltpu.SemaphoreType.DMA((2,))],
        compiler_params=params(4),
        cost_estimate=spent(20),
        name="code",
    )(in_hbm(cd_first.reshape(lines, LANES)), in_hbm(cd_second.reshape(lines, LANES)))
    coded = lax.all_to_all(coded, "cd", split_axis=0, concat_axis=0, tiled=True)

    table = jnp.transpose(amplitudes, (1, 0, 2))
    if pairs != pair_block:
        table = jnp.pad(table, ((0, 0), (0, pairs - pair_block), (0, 0)))
    table = table.reshape(orbits * pairs, orbitals)
    packed_rows = orbits // group * pairs
    steps = 10 if orbits // group % 10 == 0 else 1
    table = pl.pallas_call(
        functools.partial(pack_kernel, slabs, orbits, group, pairs),
        out_shape=jax.ShapeDtypeStruct((slabs, packed_rows, DEPTH), jnp.bfloat16),
        in_specs=[HBM],
        out_specs=VMEM,
        scratch_shapes=[
            pltpu.VMEM((orbits * pairs, orbitals), jnp.bfloat16),
            pltpu.SemaphoreType.DMA((steps,)),
        ],
        compiler_params=params(16),
        cost_estimate=cost(0, 4 * orbits * pairs * orbitals),
        name="pack",
    )(in_hbm(table))

    lookup_flops = 2 * packed_rows * DEPTH * columns
    lookup_bytes = packed_rows * DEPTH * 2 + columns * pairs * 2

    def direct_for(part, *old):
        return pl.pallas_call(
            functools.partial(direct_kernel if old else direct_first, group, pairs, shift, orbits, slabs, shares[part]),
            out_shape=jax.ShapeDtypeStruct((pairs, columns), jnp.bfloat16),
            in_specs=[VMEM] * 2 + [VMEM, ANY][: len(old)],
            out_specs=VMEM,
            compiler_params=params(20),
            cost_estimate=SMALL if old else spent(2),
            name="direct",
        )(table, own_coded, *old)

    half = slabs // 2
    first = [half - half // 4 if k < half else 0 for k in range(slabs)]
    early = {0: first[0], 1: first[0] // 2, half: half // 2}
    second = [early.get(k, 0) for k in range(slabs)]
    shares = [
        [(k, k + first[k]) for k in range(slabs)],
        [(k + first[k], k + first[k] + second[k]) for k in range(slabs)],
        [(k + first[k] + second[k], slabs) for k in range(slabs)],
    ]
    direct = direct_for(0)
    coded, direct = lax.optimization_barrier((coded, direct))

    def crossed_for(masks, name, *after):
        return pl.pallas_call(
            functools.partial(crossed_kernel, group, pairs, shift, orbits, masks),
            out_shape=jax.ShapeDtypeStruct((len(masks), pairs, columns), jnp.bfloat16),
            in_specs=[VMEM] * 2 + [ANY] * len(after),
            out_specs=VMEM,
            compiler_params=params(20),
            cost_estimate=SMALL,
            name=name,
        )(table, coded, *after)

    pairs_of = [near[at : at + 2] for at in reversed(range(0, slabs // 2, 2))]
    arrived, last = [], ()
    for masks in pairs_of:
        if arrived:
            direct = direct_for(1, direct, *last)
            last = (direct,)
        last = (crossed_for([mask + 1 for mask in masks], "crossed_far", *last),)
        arrived.append(swap(last[0], "cd", slabs, 1))
    got = []
    for masks, block in zip(pairs_of, arrived):
        merged = crossed_for(masks, "crossed_near", *last) + block
        last = (merged,)
        for k in reversed(range(len(masks))):
            if masks[k]:
                got.append(swap(merged[k], "cd", slabs, masks[k]))
    direct = direct_for(2, direct, *last)
    crossed = add_up(merged[0].astype(jnp.float32), got, 0.5)
    live_cols, _ = lax.optimization_barrier((live_cols, merged))
    slots = jnp.arange(columns, dtype=jnp.int32)
    live = (slots < live_cols[0]).astype(jnp.float32)
    weight = jnp.where(cd_first == cd_second, jnp.float32(0.5), jnp.float32(1.0)) * live
    packed = ((direct.astype(jnp.float32) + crossed) * weight[None, :]).astype(jnp.bfloat16)

    gathered = [lax.all_gather(packed[:pair_block], "ab", axis=0, tiled=True)]
    all_pairs = blocks * pair_block

    width = rows // slabs

    def ladder_for(masks, dtype, name, *after):
        return pl.pallas_call(
            functools.partial(ladder_kernel, masks, len(gathered)),
            out_shape=jax.ShapeDtypeStruct((len(masks), all_pairs, width), dtype),
            in_specs=[VMEM] * (len(gathered) + 1) + [ANY] * len(after),
            out_specs=VMEM,
            compiler_params=params(16),
            cost_estimate=SMALL,
            name=name,
        )(*gathered, pair_values, *after)

    arrived, last = [], ()
    for masks in pairs_of:
        last = (ladder_for([mask + 1 for mask in masks], jnp.bfloat16, "ladder_far", *last),)
        arrived.append(swap(last[0], "cd", slabs, 1))
    got = []
    for masks, block in zip(pairs_of, arrived):
        own = ladder_for(masks, jnp.float32, "ladder_near", *last)
        last = (own,)
        merged = own + block.astype(jnp.float32)
        sent = merged.astype(jnp.bfloat16)
        for k in reversed(range(len(masks))):
            if masks[k]:
                got.append(swap(sent[k], "cd", slabs, masks[k]))
    return add_up(merged[0], got, 0.02).astype(jnp.bfloat16)


def solution(mesh):
    placed = (P("ab", "cd"), P("ab", "cd", None), P("cd"), P("cd"), P("cd"))
    return jax.shard_map(
        on_device, mesh=mesh, in_specs=placed, out_specs=P(None, ("ab", "cd")), check_vma=False
    )
```
